256 devices in a mesh: side: 2 (over core), gx: 16 (over z, x_lo), gy: 8 (over y, x_hi).
Axes of the slice: x: 4 (x_hi: 2, x_lo: 2; x = x_hi * 2 + x_lo), y: 4, z: 8, core: 2. Of those that a mesh axis runs over, the one named last changes fastest.
Arguments:
- fields: float32 [2, 3, 16, 256, 2048], P('side', None, None, 'gx', 'gy'), may hold values from -6 to 6
- source: float32 [2, 3, 16, 256, 2048], P('side', None, None, 'gx', 'gy'), may hold values from -12 to 12
- reaction: float32 [2, 16, 256, 2048], P('side', None, 'gx', 'gy'), may hold values from 0.25 to 4
- velocity: float32 [2, 16, 256, 2048], P('side', None, 'gx', 'gy'), may hold values from 0.5 to 6
- coupling: float32 [2, 3, 3], P('side'), may hold values from -0.5 to 0.5
Outputs:
- new_fields: float32 [2, 3, 16, 256, 2048], P('side', None, None, 'gx', 'gy')
- interface: float32 [2, 3, 256, 2048], P('side', None, 'gx', 'gy')
The draws below stay inside these ranges and needn't reach their ends.
All inputs are finite; a program needn't handle non-finite values.
Results may differ from the reference program's by a relative error of at most 0.00002.
Values sent between devices are 32-bit elements; how exact they have to be, the bound alone decides.
A program may use at most 64 MiB of HBM per device.

```python
import math
import jax
import jax.numpy as jnp

K = 3
L = 16
SWEEPS = 4
NX = 256
NY = 2048


def block_levels(stream_key, extent, pieces, smallest, largest):
    level, own = 1.0, jax.random.fold_in(stream_key, 6)
    for dim, blocks in pieces:
        steps = jnp.exp(jax.random.uniform(jax.random.fold_in(own, dim), (blocks,), jnp.float32, smallest / len(pieces), largest / len(pieces)))
        level = level * jnp.repeat(steps, extent[dim] // blocks).reshape([-1 if axis == dim else 1 for axis in range(len(extent))])
    return level


def centred(key, dims, width, most, shards=(), kind=jnp.bfloat16):
    values = jax.random.normal(key, dims, jnp.float32) * width
    if len(shards) > 0:
        values = block_levels(key, dims, shards, -0.22, 0.18) * values
    return jnp.clip(values, min=-most, max=most).astype(kind)


def setup_inputs(seed: int = 0) -> dict:
    streams_of = jax.random.split(jax.random.key(seed), 6)
    return {
        "fields": centred(streams_of[0], (2, K, L, NX, NY), 1.0, 6.0, ((0, 2), (3, 16), (4, 8)), jnp.float32),
        "source": centred(streams_of[1], (2, K, L, NX, NY), 2.0, 12.0, ((0, 2), (3, 16), (4, 8)), jnp.float32),
        "reaction": jnp.clip(jnp.exp(math.log(4.0) - 2.7725887 * jax.random.uniform(streams_of[2], (2, L, NX, NY), jnp.float32) ** block_levels(streams_of[2], (2, L, NX, NY), ((0, 2), (2, 16), (3, 8)), -0.2, 0.2)), 0.25, 4.0),
        "velocity": jnp.clip(jnp.exp(math.log(6.0) - 2.4849066 * jax.random.uniform(streams_of[3], (2, L, NX, NY), jnp.float32) ** block_levels(streams_of[3], (2, L, NX, NY), ((0, 2), (2, 16), (3, 8)), -0.2, 0.2)), 0.5, 6.0),
        "coupling": jnp.clip(jax.random.uniform(streams_of[4], (2, K, K), jnp.float32, -0.5, 0.5) * block_levels(streams_of[4], (2, K, K), ((0, 2),), -0.4, 0.0), -0.5, 0.5),
    }


OMEGA = 0.8
RATIO = 0.5
THETA = 0.7


def relax(center, west_cells, east_cells, south_cells, north_cells, source, reaction, velocity, coupling, ghost_layer):
    zero_layer = jnp.zeros_like(center[:, :1])
    below = jnp.concatenate([ghost_layer[:, None], center[:, :-1]], axis=1)
    above = jnp.concatenate([center[:, 1:], zero_layer], axis=1)
    beside_all = below + above + west_cells + east_cells + south_cells + north_cells
    diag_term = 6.0 + reaction + velocity
    mixing = jnp.zeros_like(center)
    for index in range(center.shape[0]):
        mixing = mixing + coupling[:, index][:, None, None, None] * center[index][None]
    residual = source - (diag_term[None] * center - beside_all - velocity[None] * west_cells + mixing)
    scale = diag_term[None] + jnp.diagonal(coupling)[:, None, None, None]
    return center + OMEGA * residual / scale


def reference(fields, source, reaction, velocity, coupling):
    results = []
    for which in range(2):
        current = fields[which]
        for step in range(SWEEPS):
            if which == 0:
                ghost_layer = fields[1][:, 0]
            else:
                ghost_layer = current[:, 0] + RATIO * (fields[0][:, 1] - fields[0][:, 0])
            west_cells = jnp.roll(current, 1, axis=2)
            east_cells = jnp.roll(current, -1, axis=2)
            padded = jnp.pad(current, ((0, 0), (0, 0), (0, 0), (1, 1)))
            current = relax(current, west_cells, east_cells, padded[..., :-2], padded[..., 2:],
                            source[which], reaction[which], velocity[which], coupling[which], ghost_layer)
        results.append(current)
    new_fields = jnp.stack(results)
    relaxed = THETA * results[1][:, 0] + (1.0 - THETA) * results[0][:, 0]
    interface = jnp.stack([relaxed, relaxed])
    return new_fields, interface
```

```python
import functools

import jax
import jax.numpy as jnp
from jax import lax
from jax.experimental import pallas as pl
from jax.experimental.pallas import tpu as pltpu
from jax.sharding import PartitionSpec as P

SWEEPS = 4
K = 3
OMEGA = 0.8
RATIO = 0.5
THETA = 0.7
LANES = 128
MESH = pl.DeviceIdType.MESH


def kernel(
    nx,
    ny,
    L,
    X,
    GROUPS,
    f_ref,
    s_ref,
    r_ref,
    v_ref,
    c_ref,
    o_ref,
    i_ref,
    F,
    S,
    RV,
    U,
    W,
    V1,
    SS,
    YO,
    YI,
    M,
    GH,
    O,
    PR,
    IO,
    f_sem,
    s_sem,
    rv_sem,
    o_sem,
    i_sem,
    xs_sem,
    xr_sem,
    ys_sem,
    yr_sem,
    p_sem,
    C,
    c_sem,
):
    side = lax.axis_index("side")
    gx = lax.axis_index("gx")
    gy = lax.axis_index("gy")
    fluid = side == 0
    west = (side, lax.rem(gx + nx - 1, nx), gy)
    east = (side, lax.rem(gx + 1, nx), gy)
    south = (side, gx, gy - 1)
    north = (side, gx, gy + 1)
    partner = (1 - side, gx, gy)
    has_south = gy > 0
    has_north = gy < ny - 1
    pairs = X // 2 // GROUPS

    barrier = pltpu.get_barrier_semaphore()

    def greet(device):
        pl.semaphore_signal(barrier, inc=1, device_id=device, device_id_type=MESH)

    greet(west)
    greet(east)
    greet(partner)
    pl.when(has_south)(lambda: greet(south))
    pl.when(has_north)(lambda: greet(north))

    def half(ref, h):
        return ref.at[..., pl.ds(h * LANES, LANES)]

    loads_f = [pltpu.make_async_copy(half(f_ref, h), F.at[h], f_sem.at[h]) for h in range(2)]
    loads_s = [pltpu.make_async_copy(half(s_ref, h), S.at[h], s_sem.at[h]) for h in range(2)]
    loads_rv = [
        pltpu.make_async_copy(half(ref, h), RV.at[n, h], rv_sem.at[n, h])
        for n, ref in enumerate((r_ref, v_ref))
        for h in range(2)
    ]
    load_c = pltpu.make_async_copy(c_ref, C, c_sem)
    for copy in loads_f + loads_rv + loads_s + [load_c]:
        copy.start()

    lane = lax.broadcasted_iota(jnp.int32, (8, LANES), 1)
    wide_lane = lax.broadcasted_iota(jnp.int32, (L, LANES), 1)
    row = lax.broadcasted_iota(jnp.int32, (L, LANES), 0)
    zero = jnp.zeros((8, LANES), jnp.float32)

    def x_copy(t, d):
        source, target = ((X, 0), (1, X + 1))[d]
        return pltpu.make_async_remote_copy(
            U.at[t, :, :, source],
            U.at[t, :, :, target],
            xs_sem.at[t, d],
            xr_sem.at[t, d],
            device_id=(east, west)[d],
            device_id_type=MESH,
        )

    def y_copy(t, g, d):
        return pltpu.make_async_remote_copy(
            YO.at[t, g, d],
            YI.at[t, g, d],
            ys_sem.at[t, g, d],
            yr_sem.at[t, g, d],
            device_id=(north, south)[d],
            device_id_type=MESH,
        )

    def y_start(t, g):
        pl.when(has_north)(lambda: y_copy(t, g, 0).start())
        pl.when(has_south)(lambda: y_copy(t, g, 1).start())

    def y_wait(t, g):
        pl.when(has_south)(lambda: y_copy(t, g, 0).wait_recv())
        pl.when(has_north)(lambda: y_copy(t, g, 1).wait_recv())

    def packed(columns, first, last, slot):
        to_north, to_south = columns
        for part in range(2):
            place = slot * 2 + part
            rows = slice(8 * part, 8 * part + 8)
            to_north = jnp.where(lane == place, pltpu.roll(last[rows], place + 1, 1), to_north)
            moved = pltpu.roll(first[rows], place, 1) if place else first[rows]
            to_south = jnp.where(lane == place, moved, to_south)
        return to_north, to_south

    def unpacked(packet, slot, target):
        parts = []
        for part in range(2):
            shift = (target - (slot * 2 + part)) % LANES
            parts.append(pltpu.roll(packet, shift, 1) if shift else packet)
        return jnp.concatenate(parts, axis=0)

    def rows_of(g):
        for n in range(pairs):
            pair = g * pairs + n
            yield pair, 2 * n
            yield X - 1 - pair, 2 * n + 1

    for copy in loads_f:
        copy.wait()

    for h in range(2):
        for k in range(K):
            layer0, layer1 = F[h, k, 0:X], F[h, k, X : 2 * X]
            M[h, k] = jnp.where(fluid, RATIO * (layer1 - layer0), layer0)

    def stage(g, carry):
        columns = (zero, zero)
        for x, number in rows_of(g):
            for k in range(K):
                tiles = []
                for h in range(2):
                    tile = jnp.concatenate(
                        [
                            F[h, k, pl.ds(8 * part * X + x, 8, stride=X), :]
                            for part in range(2)
                        ],
                        axis=0,
                    )
                    U[0, h, k, x + 1] = tile
                    tiles.append(tile)
                columns = packed(columns, tiles[0], tiles[1], number * K + k)
        YO[0, g, 0], YO[0, g, 1] = columns
        return carry

    lax.fori_loop(0, GROUPS, stage, 0)

    greeted = 3 + has_south.astype(jnp.int32) + has_north.astype(jnp.int32)
    pl.semaphore_wait(barrier, greeted)

    for g in range(GROUPS):
        y_start(0, g)
    for d in range(2):
        x_copy(0, d).start()
    ghosts = pltpu.make_async_remote_copy(
        M, GH, p_sem.at[0], p_sem.at[1], device_id=partner, device_id_type=MESH
    )
    ghosts.start()

    def blank(d):
        for t in range(SWEEPS):
            for g in range(GROUPS):
                YI[t, g, d] = zero

    pl.when(jnp.logical_not(has_south))(lambda: blank(0))
    pl.when(jnp.logical_not(has_north))(lambda: blank(1))

    for copy in loads_rv + loads_s + [load_c]:
        copy.wait()
    mix = [[C[k, 0, j] for j in range(K)] for k in range(K)]

    def weigh(x, carry):
        for h in range(2):
            for part in range(2):
                rows = pl.ds(8 * part * X + x, 8, stride=X)
                out = pl.ds(8 * part, 8)
                speed = RV[1, h, rows, :]
                diag = 6.0 + RV[0, h, rows, :] + speed
                V1[h, x, out] = 1.0 + speed
                for k in range(K):
                    W[h, k, x, out] = OMEGA / (diag + mix[k][k])
                    SS[h, k, x, out] = S[h, k, rows, :]
        return carry

    lax.fori_loop(0, X, weigh, 0)

    ghosts.wait()
    own = jnp.where(fluid, 0.0, 1.0)

    def relax(t, g, x, number):
        speeds = [V1[h, x] for h in range(2)]
        center = [[U[t, h, k, x + 1] for h in range(2)] for k in range(K)]
        new = []
        for k in range(K):
            slot = number * K + k
            from_south = unpacked(YI[t, g, 0], slot, 0)
            from_north = unpacked(YI[t, g, 1], slot, LANES - 1)
            up = [pltpu.roll(center[k][h], 1, 1) for h in range(2)]
            down = [pltpu.roll(center[k][h], LANES - 1, 1) for h in range(2)]
            souths = (
                jnp.where(wide_lane == 0, from_south, up[0]),
                jnp.where(wide_lane == 0, up[0], up[1]),
            )
            norths = (
                jnp.where(wide_lane == LANES - 1, down[1], down[0]),
                jnp.where(wide_lane == LANES - 1, from_north, down[1]),
            )
            results = []
            for h in range(2):
                here = center[k][h]
                ghost = own * here + GH[h, k, pl.ds(x, 1), :]
                below = jnp.where(row == 0, ghost, pltpu.roll(here, 1, 0))
                above = jnp.where(row == L - 1, 0.0, pltpu.roll(here, L - 1, 0))
                total = SS[h, k, x] + below + above
                total = total + speeds[h] * U[t, h, k, x] + U[t, h, k, x + 2]
                total = total + souths[h] + norths[h]
                for j in range(K):
                    if j != k:
                        total = total - mix[k][j] * center[j][h]
                results.append((1.0 - OMEGA) * here + W[h, k, x] * total)
            new.append(results)
        return new

    def sweep(t, carry):
        for d in range(2):
            x_copy(t, d).wait_recv()

        def group(g, carry):
            y_wait(t, g)
            columns = (zero, zero)
            for x, number in rows_of(g):
                new = relax(t, g, x, number)
                for k in range(K):
                    for h in range(2):
                        U[t + 1, h, k, x + 1] = new[k][h]
                    columns = packed(columns, new[k][0], new[k][1], number * K + k)
                if number == 1:

                    @pl.when(g == 0)
                    def _():
                        for d in range(2):
                            x_copy(t + 1, d).start()

            YO[t + 1, g, 0], YO[t + 1, g, 1] = columns
            y_start(t + 1, g)
            return carry

        lax.fori_loop(0, GROUPS, group, 0)
        return carry

    lax.fori_loop(0, SWEEPS - 1, sweep, 0)

    last = SWEEPS - 1
    for d in range(2):
        x_copy(last, d).wait_recv()

    def finish(g, carry):
        y_wait(last, g)
        for x, number in rows_of(g):
            new = relax(last, g, x, number)
            for k in range(K):
                for h in range(2):
                    for part in range(2):
                        rows = pl.ds(8 * part * X + x, 8, stride=X)
                        O[h, k, rows, :] = new[k][h][8 * part : 8 * part + 8]
        return carry

    lax.fori_loop(0, GROUPS, finish, 0)

    traces = pltpu.make_async_remote_copy(
        O.at[:, :, pl.ds(0, X)], PR, p_sem.at[2], p_sem.at[3], device_id=partner, device_id_type=MESH
    )
    traces.start()
    stores = [pltpu.make_async_copy(O.at[h], half(o_ref, h), o_sem.at[h]) for h in range(2)]
    for copy in stores:
        copy.start()

    for t in range(SWEEPS):
        for d in range(2):
            x_copy(t, d).wait_send()

    def sent(n, carry):
        t, g = n // GROUPS, lax.rem(n, GROUPS)
        pl.when(has_north)(lambda: y_copy(t, g, 0).wait_send())
        pl.when(has_south)(lambda: y_copy(t, g, 1).wait_send())
        return carry

    lax.fori_loop(0, SWEEPS * GROUPS, sent, 0)

    traces.wait()
    mine = jnp.where(fluid, 1.0 - THETA, THETA)
    other = jnp.where(fluid, THETA, 1.0 - THETA)
    for h in range(2):
        for k in range(K):
            IO[h, k] = mine * O[h, k, 0:X] + other * PR[h, k]
    edges = [pltpu.make_async_copy(IO.at[h], half(i_ref, h), i_sem.at[h]) for h in range(2)]
    for copy in edges:
        copy.start()
    for copy in stores + edges:
        copy.wait()


def solution(mesh):
    nx, ny = mesh.shape["gx"], mesh.shape["gy"]

    def local(fields, source, reaction, velocity, coupling):
        _, _, L, X, Y = fields.shape
        groups = 4
        f32 = jnp.float32
        cells = L * X
        new, interface = pl.pallas_call(
            functools.partial(kernel, nx, ny, L, X, groups),
            out_shape=(
                jax.ShapeDtypeStruct((K, cells, Y), f32),
                jax.ShapeDtypeStruct((K, X, Y), f32),
            ),
            in_specs=[pl.BlockSpec(memory_space=pltpu.HBM)] * 5,
            out_specs=[pl.BlockSpec(memory_space=pl.ANY)] * 2,
            scratch_shapes=[
                pltpu.VMEM((2, K, cells, LANES), f32),
                pltpu.VMEM((2, K, cells, LANES), f32),
                pltpu.VMEM((2, 2, cells, LANES), f32),
                pltpu.VMEM((SWEEPS, 2, K, X + 2, L, LANES), f32),
                pltpu.VMEM((2, K, X, L, LANES), f32),
                pltpu.VMEM((2, X, L, LANES), f32),
                pltpu.VMEM((2, K, X, L, LANES), f32),
                pltpu.VMEM((SWEEPS, groups, 2, 8, LANES), f32),
                pltpu.VMEM((SWEEPS, groups, 2, 8, LANES), f32),
                pltpu.VMEM((2, K, X, LANES), f32),
                pltpu.VMEM((2, K, X, LANES), f32),
                pltpu.VMEM((2, K, cells, LANES), f32),
                pltpu.VMEM((2, K, X, LANES), f32),
                pltpu.VMEM((2, K, X, LANES), f32),
                pltpu.SemaphoreType.DMA((2,)),
                pltpu.SemaphoreType.DMA((2,)),
                pltpu.SemaphoreType.DMA((2, 2)),
                pltpu.SemaphoreType.DMA((2,)),
                pltpu.SemaphoreType.DMA((2,)),
                pltpu.SemaphoreType.DMA((SWEEPS, 2)),
                pltpu.SemaphoreType.DMA((SWEEPS, 2)),
                pltpu.SemaphoreType.DMA((SWEEPS, groups, 2)),
                pltpu.SemaphoreType.DMA((SWEEPS, groups, 2)),
                pltpu.SemaphoreType.DMA((4,)),
                pltpu.SMEM((K, 1, K), f32),
                pltpu.SemaphoreType.DMA,
            ],
            compiler_params=pltpu.CompilerParams(
                collective_id=0,
                has_side_effects=True,
                vmem_limit_bytes=60 * 1024 * 1024,
            ),
        )(
            fields.reshape(K, cells, Y),
            source.reshape(K, cells, Y),
            reaction.reshape(cells, Y),
            velocity.reshape(cells, Y),
            coupling.reshape(K, 1, K),
        )
        return new.reshape(1, K, L, X, Y), interface[None]

    return jax.shard_map(
        local,
        mesh=mesh,
        in_specs=(
            P("side", None, None, "gx", "gy"),
            P("side", None, None, "gx", "gy"),
            P("side", None, "gx", "gy"),
            P("side", None, "gx", "gy"),
            P("side", None, None),
        ),
        out_specs=(P("side", None, None, "gx", "gy"), P("side", None, "gx", "gy")),
        check_vma=False,
    )
```

```python
import functools

import jax
import jax.numpy as jnp
from jax import lax
from jax.experimental import pallas as pl
from jax.experimental.pallas import tpu as pltpu
from jax.sharding import PartitionSpec as P

SWEEPS = 4
K = 3
OMEGA = 0.8
RATIO = 0.5
THETA = 0.7
LANES = 128
MESH = pl.DeviceIdType.MESH


def kernel(
    nx,
    ny,
    L,
    X,
    SPANS,
    f_ref,
    s_ref,
    r_ref,
    v_ref,
    c_ref,
    O,
    IO,
    F,
    S,
    RV,
    U,
    W,
    V1,
    SS,
    YO,
    YI,
    M,
    GH,
    PR,
    f_sem,
    s_sem,
    rv_sem,
    xs_sem,
    xr_sem,
    ys_sem,
    yr_sem,
    p_sem,
    C,
    c_sem,
):
    side = lax.axis_index("side")
    gx = lax.axis_index("gx")
    gy = lax.axis_index("gy")
    fluid = side == 0
    west = (side, lax.rem(gx + nx - 1, nx), gy)
    east = (side, lax.rem(gx + 1, nx), gy)
    south = (side, gx, gy - 1)
    north = (side, gx, gy + 1)
    partner = (1 - side, gx, gy)
    has_south = gy > 0
    has_north = gy < ny - 1
    groups = len(SPANS)

    barrier = pltpu.get_barrier_semaphore()

    def greet(device):
        pl.semaphore_signal(barrier, inc=1, device_id=device, device_id_type=MESH)

    greet(west)
    greet(east)
    greet(partner)
    pl.when(has_south)(lambda: greet(south))
    pl.when(has_north)(lambda: greet(north))

    def half(ref, h):
        return ref.at[..., pl.ds(h * LANES, LANES)]

    loads_f = [pltpu.make_async_copy(half(f_ref, h), F.at[h], f_sem.at[h]) for h in range(2)]
    loads_s = [pltpu.make_async_copy(half(s_ref, h), S.at[h], s_sem.at[h]) for h in range(2)]
    loads_rv = [
        pltpu.make_async_copy(half(ref, h), RV.at[n, h], rv_sem.at[n, h])
        for n, ref in enumerate((r_ref, v_ref))
        for h in range(2)
    ]
    load_c = pltpu.make_async_copy(c_ref, C, c_sem)
    for copy in loads_f + loads_rv + loads_s + [load_c]:
        copy.start()

    lane = lax.broadcasted_iota(jnp.int32, (8, LANES), 1)
    wide_lane = lax.broadcasted_iota(jnp.int32, (L, LANES), 1)
    row = lax.broadcasted_iota(jnp.int32, (L, LANES), 0)
    zero = jnp.zeros((8, LANES), jnp.float32)

    def x_copy(t, d):
        source, target = ((X, 0), (1, X + 1))[d]
        return pltpu.make_async_remote_copy(
            U.at[t, :, :, source],
            U.at[t, :, :, target],
            xs_sem.at[t, d],
            xr_sem.at[t, d],
            device_id=(east, west)[d],
            device_id_type=MESH,
        )

    def y_copy(t, g, d):
        return pltpu.make_async_remote_copy(
            YO.at[t, g, d],
            YI.at[t, g, d],
            ys_sem.at[t, g, d],
            yr_sem.at[t, g, d],
            device_id=(north, south)[d],
            device_id_type=MESH,
        )

    def x_both(t, step):
        for d in range(2):
            getattr(x_copy(t, d), step)()

    def y_start(t, g):
        pl.when(has_north)(lambda: y_copy(t, g, 0).start())
        pl.when(has_south)(lambda: y_copy(t, g, 1).start())

    def y_wait(t, g):
        pl.when(has_south)(lambda: y_copy(t, g, 0).wait_recv())
        pl.when(has_north)(lambda: y_copy(t, g, 1).wait_recv())

    def sent(t):
        x_both(t, "wait_send")
        for g in range(groups):
            pl.when(has_north)(lambda: y_copy(t, g, 0).wait_send())
            pl.when(has_south)(lambda: y_copy(t, g, 1).wait_send())

    def packed(columns, first, last, slot):
        to_north, to_south = columns
        for part in range(2):
            place = slot * 2 + part
            rows = slice(8 * part, 8 * part + 8)
            to_north = jnp.where(lane == place, pltpu.roll(last[rows], place + 1, 1), to_north)
            moved = pltpu.roll(first[rows], place, 1) if place else first[rows]
            to_south = jnp.where(lane == place, moved, to_south)
        return to_north, to_south

    def unpacked(packet, slot, target):
        parts = []
        for part in range(2):
            shift = (target - (slot * 2 + part)) % LANES
            parts.append(pltpu.roll(packet, shift, 1) if shift else packet)
        return jnp.concatenate(parts, axis=0)

    def rows_of(g):
        start = sum(SPANS[:g])
        for n in range(SPANS[g]):
            yield start + n, 2 * n
            yield X - 1 - start - n, 2 * n + 1

    for copy in loads_f:
        copy.wait()

    for h in range(2):
        for k in range(K):
            layer0, layer1 = F[h, k, 0:X], F[h, k, X : 2 * X]
            M[h, k] = jnp.where(fluid, RATIO * (layer1 - layer0), layer0)

    for g in range(groups):
        columns = (zero, zero)
        for x, number in rows_of(g):
            for k in range(K):
                tiles = []
                for h in range(2):
                    tile = jnp.concatenate(
                        [
                            F[h, k, pl.ds(8 * part * X + x, 8, stride=X), :]
                            for part in range(2)
                        ],
                        axis=0,
                    )
                    U[0, h, k, x + 1] = tile
                    tiles.append(tile)
                columns = packed(columns, tiles[0], tiles[1], number * K + k)
        YO[0, g, 0], YO[0, g, 1] = columns

    greeted = 3 + has_south.astype(jnp.int32) + has_north.astype(jnp.int32)
    pl.semaphore_wait(barrier, greeted)

    for g in range(groups):
        y_start(0, g)
    x_both(0, "start")
    ghosts = pltpu.make_async_remote_copy(
        M, GH, p_sem.at[0], p_sem.at[1], device_id=partner, device_id_type=MESH
    )
    ghosts.start()

    def blank(d):
        for t in range(SWEEPS):
            for g in range(groups):
                YI[t, g, d] = zero

    pl.when(jnp.logical_not(has_south))(lambda: blank(0))
    pl.when(jnp.logical_not(has_north))(lambda: blank(1))

    for copy in loads_rv + loads_s + [load_c]:
        copy.wait()
    mix = [[C[k, 0, j] for j in range(K)] for k in range(K)]

    def weigh(x, carry):
        for h in range(2):
            for part in range(2):
                rows = pl.ds(8 * part * X + x, 8, stride=X)
                out = pl.ds(8 * part, 8)
                speed = RV[1, h, rows, :]
                diag = 6.0 + RV[0, h, rows, :] + speed
                V1[h, x, out] = 1.0 + speed
                for k in range(K):
                    W[h, k, x, out] = OMEGA / (diag + mix[k][k])
                    SS[h, k, x, out] = S[h, k, rows, :]
        return carry

    lax.fori_loop(0, X, weigh, 0)

    ghosts.wait()
    own = jnp.where(fluid, 0.0, 1.0)

    def relax(t, g, x, number):
        speeds = [V1[h, x] for h in range(2)]
        center = [[U[t, h, k, x + 1] for h in range(2)] for k in range(K)]
        new = []
        for k in range(K):
            slot = number * K + k
            from_south = unpacked(YI[t, g, 0], slot, 0)
            from_north = unpacked(YI[t, g, 1], slot, LANES - 1)
            up = [pltpu.roll(center[k][h], 1, 1) for h in range(2)]
            down = [pltpu.roll(center[k][h], LANES - 1, 1) for h in range(2)]
            souths = (
                jnp.where(wide_lane == 0, from_south, up[0]),
                jnp.where(wide_lane == 0, up[0], up[1]),
            )
            norths = (
                jnp.where(wide_lane == LANES - 1, down[1], down[0]),
                jnp.where(wide_lane == LANES - 1, from_north, down[1]),
            )
            results = []
            for h in range(2):
                here = center[k][h]
                ghost = own * here + GH[h, k, pl.ds(x, 1), :]
                below = jnp.where(row == 0, ghost, pltpu.roll(here, 1, 0))
                above = jnp.where(row == L - 1, 0.0, pltpu.roll(here, L - 1, 0))
                total = SS[h, k, x] + below + above
                total = total + speeds[h] * U[t, h, k, x] + U[t, h, k, x + 2]
                total = total + souths[h] + norths[h]
                for j in range(K):
                    if j != k:
                        total = total - mix[k][j] * center[j][h]
                results.append((1.0 - OMEGA) * here + W[h, k, x] * total)
            new.append(results)
        return new

    def sweep(t, carry):
        for g in range(groups):
            y_wait(t, g)
            if g == 0:
                x_both(t, "wait_recv")
            columns = (zero, zero)
            for x, number in rows_of(g):
                new = relax(t, g, x, number)
                for k in range(K):
                    for h in range(2):
                        U[t + 1, h, k, x + 1] = new[k][h]
                    columns = packed(columns, new[k][0], new[k][1], number * K + k)
                if g == 0 and number == 1:
                    x_both(t + 1, "start")
            YO[t + 1, g, 0], YO[t + 1, g, 1] = columns
            y_start(t + 1, g)
        sent(t)
        return carry

    lax.fori_loop(0, SWEEPS - 1, sweep, 0)

    last = SWEEPS - 1
    for g in range(groups):
        y_wait(last, g)
        if g == 0:
            x_both(last, "wait_recv")
        for x, number in rows_of(g):
            new = relax(last, g, x, number)
            for k in range(K):
                for h in range(2):
                    for part in range(2):
                        rows = pl.ds(8 * part * X + x, 8, stride=X)
                        O[h, k, rows, :] = new[k][h][8 * part : 8 * part + 8]

    traces = pltpu.make_async_remote_copy(
        O.at[:, :, pl.ds(0, X)], PR, p_sem.at[2], p_sem.at[3], device_id=partner, device_id_type=MESH
    )
    traces.start()
    sent(last)
    traces.wait()
    mine = jnp.where(fluid, 1.0 - THETA, THETA)
    other = jnp.where(fluid, THETA, 1.0 - THETA)
    for h in range(2):
        for k in range(K):
            IO[h, k] = mine * O[h, k, 0:X] + other * PR[h, k]


def write(a_ref, b_ref, o_ref, i_ref, sem):
    copies = [
        pltpu.make_async_copy(
            tile_ref.at[h], out_ref.at[..., pl.ds(h * LANES, LANES)], sem.at[n, h]
        )
        for n, (tile_ref, out_ref) in enumerate(((a_ref, o_ref), (b_ref, i_ref)))
        for h in range(2)
    ]
    for copy in copies:
        copy.start()
    for copy in copies:
        copy.wait()


def solution(mesh):
    nx, ny = mesh.shape["gx"], mesh.shape["gy"]

    def local(fields, source, reaction, velocity, coupling):
        _, _, L, X, Y = fields.shape
        spans = (2, 6)
        groups = len(spans)
        f32 = jnp.float32
        cells = L * X
        tiles, edges = pl.pallas_call(
            functools.partial(kernel, nx, ny, L, X, spans),
            out_shape=(
                pltpu.VMEM((2, K, cells, LANES), f32),
                pltpu.VMEM((2, K, X, LANES), f32),
            ),
            in_specs=[pl.BlockSpec(memory_space=pltpu.HBM)] * 5,
            out_specs=[pl.BlockSpec(memory_space=pltpu.VMEM)] * 2,
            scratch_shapes=[
                pltpu.VMEM((2, K, cells, LANES), f32),
                pltpu.VMEM((2, K, cells, LANES), f32),
                pltpu.VMEM((2, 2, cells, LANES), f32),
                pltpu.VMEM((SWEEPS, 2, K, X + 2, L, LANES), f32),
                pltpu.VMEM((2, K, X, L, LANES), f32),
                pltpu.VMEM((2, X, L, LANES), f32),
                pltpu.VMEM((2, K, X, L, LANES), f32),
                pltpu.VMEM((SWEEPS, groups, 2, 8, LANES), f32),
                pltpu.VMEM((SWEEPS, groups, 2, 8, LANES), f32),
                pltpu.VMEM((2, K, X, LANES), f32),
                pltpu.VMEM((2, K, X, LANES), f32),
                pltpu.VMEM((2, K, X, LANES), f32),
                pltpu.SemaphoreType.DMA((2,)),
                pltpu.SemaphoreType.DMA((2,)),
                pltpu.SemaphoreType.DMA((2, 2)),
                pltpu.SemaphoreType.DMA((SWEEPS, 2)),
                pltpu.SemaphoreType.DMA((SWEEPS, 2)),
                pltpu.SemaphoreType.DMA((SWEEPS, groups, 2)),
                pltpu.SemaphoreType.DMA((SWEEPS, groups, 2)),
                pltpu.SemaphoreType.DMA((4,)),
                pltpu.SMEM((K, 1, K), f32),
                pltpu.SemaphoreType.DMA,
            ],
            compiler_params=pltpu.CompilerParams(
                collective_id=0,
                has_side_effects=True,
                vmem_limit_bytes=60 * 1024 * 1024,
            ),
        )(
            fields.reshape(K, cells, Y),
            source.reshape(K, cells, Y),
            reaction.reshape(cells, Y),
            velocity.reshape(cells, Y),
            coupling.reshape(K, 1, K),
        )
        tiles, edges = (
            pltpu.with_memory_space_constraint(value, pltpu.VMEM) for value in (tiles, edges)
        )
        new, interface = pl.pallas_call(
            write,
            out_shape=(
                jax.ShapeDtypeStruct((K, cells, Y), f32),
                jax.ShapeDtypeStruct((K, X, Y), f32),
            ),
            in_specs=[pl.BlockSpec(memory_space=pltpu.VMEM)] * 2,
            out_specs=[pl.BlockSpec(memory_space=pltpu.HBM)] * 2,
            scratch_shapes=[pltpu.SemaphoreType.DMA((2, 2))],
        )(tiles, edges)
        return new.reshape(1, K, L, X, Y), interface[None]

    return jax.shard_map(
        local,
        mesh=mesh,
        in_specs=(
            P("side", None, None, "gx", "gy"),
            P("side", None, None, "gx", "gy"),
            P("side", None, "gx", "gy"),
            P("side", None, "gx", "gy"),
            P("side", None, None),
        ),
        out_specs=(P("side", None, None, "gx", "gy"), P("side", None, "gx", "gy")),
        check_vma=False,
    )
```

```python
import functools

import jax
import jax.numpy as jnp
from jax import lax
from jax.experimental import pallas as pl
from jax.experimental.pallas import tpu as pltpu
from jax.sharding import PartitionSpec as P

SWEEPS = 4
K = 3
OMEGA = 0.8
RATIO = 0.5
THETA = 0.7
LANES = 128
MESH = pl.DeviceIdType.MESH


def kernel(
    nx,
    ny,
    L,
    X,
    SPANS,
    f_ref,
    s_ref,
    r_ref,
    v_ref,
    c_ref,
    O,
    IO,
    F,
    S,
    RV,
    U,
    W,
    V1,
    SS,
    YO,
    YI,
    M,
    GH,
    PR,
    f_sem,
    s_sem,
    rv_sem,
    xs_sem,
    xr_sem,
    ys_sem,
    yr_sem,
    p_sem,
    C,
    c_sem,
):
    side = lax.axis_index("side")
    gx = lax.axis_index("gx")
    gy = lax.axis_index("gy")
    fluid = side == 0
    west = (side, lax.rem(gx + nx - 1, nx), gy)
    east = (side, lax.rem(gx + 1, nx), gy)
    south = (side, gx, gy - 1)
    north = (side, gx, gy + 1)
    partner = (1 - side, gx, gy)
    has_south = gy > 0
    has_north = gy < ny - 1
    groups = len(SPANS)

    barrier = pltpu.get_barrier_semaphore()

    def greet(device):
        pl.semaphore_signal(barrier, inc=1, device_id=device, device_id_type=MESH)

    greet(west)
    greet(east)
    greet(partner)
    pl.when(has_south)(lambda: greet(south))
    pl.when(has_north)(lambda: greet(north))

    def half(ref, h):
        return ref.at[..., pl.ds(h * LANES, LANES)]

    loads_f = [pltpu.make_async_copy(half(f_ref, h), F.at[h], f_sem.at[h]) for h in range(2)]
    loads_s = [pltpu.make_async_copy(half(s_ref, h), S.at[h], s_sem.at[h]) for h in range(2)]
    loads_rv = [
        pltpu.make_async_copy(half(ref, h), RV.at[n, h], rv_sem.at[n, h])
        for n, ref in enumerate((r_ref, v_ref))
        for h in range(2)
    ]
    load_c = pltpu.make_async_copy(c_ref, C, c_sem)
    for copy in loads_f + loads_rv + loads_s + [load_c]:
        copy.start()

    lane = lax.broadcasted_iota(jnp.int32, (8, LANES), 1)
    wide_lane = lax.broadcasted_iota(jnp.int32, (L, LANES), 1)
    row = lax.broadcasted_iota(jnp.int32, (L, LANES), 0)
    zero = jnp.zeros((8, LANES), jnp.float32)

    def x_copy(t, d):
        source, target = ((X, 0), (1, X + 1))[d]
        return pltpu.make_async_remote_copy(
            U.at[t, source],
            U.at[t, target],
            xs_sem.at[t, d],
            xr_sem.at[t, d],
            device_id=(east, west)[d],
            device_id_type=MESH,
        )

    def y_copy(t, g, d):
        return pltpu.make_async_remote_copy(
            YO.at[t, g, d],
            YI.at[t, g, d],
            ys_sem.at[t, g, d],
            yr_sem.at[t, g, d],
            device_id=(north, south)[d],
            device_id_type=MESH,
        )

    def x_both(t, step):
        for d in range(2):
            getattr(x_copy(t, d), step)()

    def y_start(t, g):
        pl.when(has_north)(lambda: y_copy(t, g, 0).start())
        pl.when(has_south)(lambda: y_copy(t, g, 1).start())

    def y_wait(t, g):
        pl.when(has_south)(lambda: y_copy(t, g, 0).wait_recv())
        pl.when(has_north)(lambda: y_copy(t, g, 1).wait_recv())

    def sent(t):
        x_both(t, "wait_send")
        for g in range(groups):
            pl.when(has_north)(lambda: y_copy(t, g, 0).wait_send())
            pl.when(has_south)(lambda: y_copy(t, g, 1).wait_send())

    def packed(columns, first, last, slot):
        to_north, to_south = columns
        for part in range(2):
            place = slot * 2 + part
            rows = slice(8 * part, 8 * part + 8)
            to_north = jnp.where(lane == place, pltpu.roll(last[rows], place + 1, 1), to_north)
            moved = pltpu.roll(first[rows], place, 1) if place else first[rows]
            to_south = jnp.where(lane == place, moved, to_south)
        return to_north, to_south

    def unpacked(packet, slot, target):
        parts = []
        for part in range(2):
            shift = lax.rem(target + LANES - (slot * 2 + part), LANES)
            parts.append(pltpu.roll(packet, shift, 1))
        return jnp.concatenate(parts, axis=0)

    def rows_of(g):
        start = sum(SPANS[:g])
        for n in range(SPANS[g]):
            yield start + n, 2 * n
            yield X - 1 - start - n, 2 * n + 1

    for copy in loads_f:
        copy.wait()

    for h in range(2):
        for k in range(K):
            layer0, layer1 = F[h, k, 0:X], F[h, k, X : 2 * X]
            M[h, k] = jnp.where(fluid, RATIO * (layer1 - layer0), layer0)

    for g in range(groups):
        columns = (zero, zero)
        for x, number in rows_of(g):
            for k in range(K):
                tiles = []
                for h in range(2):
                    tile = jnp.concatenate(
                        [
                            F[h, k, pl.ds(8 * part * X + x, 8, stride=X), :]
                            for part in range(2)
                        ],
                        axis=0,
                    )
                    U[0, x + 1, h, k] = tile
                    tiles.append(tile)
                columns = packed(columns, tiles[0], tiles[1], number * K + k)
        YO[0, g, 0], YO[0, g, 1] = columns

    greeted = 3 + has_south.astype(jnp.int32) + has_north.astype(jnp.int32)
    pl.semaphore_wait(barrier, greeted)

    for g in range(groups):
        y_start(0, g)
    x_both(0, "start")
    ghosts = pltpu.make_async_remote_copy(
        M, GH, p_sem.at[0], p_sem.at[1], device_id=partner, device_id_type=MESH
    )
    ghosts.start()

    def blank(d):
        for t in range(SWEEPS):
            for g in range(groups):
                YI[t, g, d] = zero

    pl.when(jnp.logical_not(has_south))(lambda: blank(0))
    pl.when(jnp.logical_not(has_north))(lambda: blank(1))

    for copy in loads_rv + loads_s + [load_c]:
        copy.wait()
    mix = [[C[k, 0, j] for j in range(K)] for k in range(K)]

    def weigh(x, carry):
        for h in range(2):
            for part in range(2):
                rows = pl.ds(8 * part * X + x, 8, stride=X)
                out = pl.ds(8 * part, 8)
                speed = RV[1, h, rows, :]
                diag = 6.0 + RV[0, h, rows, :] + speed
                V1[h, x, out] = 1.0 + speed
                for k in range(K):
                    W[h, k, x, out] = OMEGA / (diag + mix[k][k])
                    SS[h, k, x, out] = S[h, k, rows, :]
        return carry

    lax.fori_loop(0, X, weigh, 0)

    ghosts.wait()
    own = jnp.where(fluid, 0.0, 1.0)

    def relax(t, g, x, number):
        speeds = [V1[h, x] for h in range(2)]
        center = [[U[t, x + 1, h, k] for h in range(2)] for k in range(K)]
        new = []
        for k in range(K):
            slot = number * K + k
            from_south = unpacked(YI[t, g, 0], slot, 0)
            from_north = unpacked(YI[t, g, 1], slot, LANES - 1)
            up = [pltpu.roll(center[k][h], 1, 1) for h in range(2)]
            down = [pltpu.roll(center[k][h], LANES - 1, 1) for h in range(2)]
            souths = (
                jnp.where(wide_lane == 0, from_south, up[0]),
                jnp.where(wide_lane == 0, up[0], up[1]),
            )
            norths = (
                jnp.where(wide_lane == LANES - 1, down[1], down[0]),
                jnp.where(wide_lane == LANES - 1, from_north, down[1]),
            )
            results = []
            for h in range(2):
                here = center[k][h]
                ghost = own * here + GH[h, k, pl.ds(x, 1), :]
                below = jnp.where(row == 0, ghost, pltpu.roll(here, 1, 0))
                above = jnp.where(row == L - 1, 0.0, pltpu.roll(here, L - 1, 0))
                total = SS[h, k, x] + below + above
                total = total + speeds[h] * U[t, x, h, k] + U[t, x + 2, h, k]
                total = total + souths[h] + norths[h]
                for j in range(K):
                    if j != k:
                        total = total - mix[k][j] * center[j][h]
                results.append((1.0 - OMEGA) * here + W[h, k, x] * total)
            new.append(results)
        return new

    def advance(t, g, x, number):
        new = relax(t, g, x, number)
        for k in range(K):
            for h in range(2):
                U[t + 1, x + 1, h, k] = new[k][h]

    def gather(t, g):
        columns = (zero, zero)
        for x, number in rows_of(g):
            for k in range(K):
                columns = packed(columns, U[t, x + 1, 0, k], U[t, x + 1, 1, k], number * K + k)
        YO[t, g, 0], YO[t, g, 1] = columns

    def sweep(t, carry):
        for g in range(groups):
            y_wait(t, g)
            start = sum(SPANS[:g])
            first = 0
            if g == 0:
                x_both(t, "wait_recv")
                advance(t, 0, 0, 0)
                advance(t, 0, X - 1, 1)
                x_both(t + 1, "start")
                first = 1

            def inwards(n, carry):
                advance(t, g, start + n, 2 * n)
                advance(t, g, X - 1 - start - n, 2 * n + 1)
                return carry

            for n in range(first, SPANS[g]):
                inwards(n, 0)
            gather(t + 1, g)
            y_start(t + 1, g)
        sent(t)
        return carry

    lax.fori_loop(0, SWEEPS - 1, sweep, 0)

    last = SWEEPS - 1
    for g in range(groups):
        y_wait(last, g)
        if g == 0:
            x_both(last, "wait_recv")
        for x, number in rows_of(g):
            new = relax(last, g, x, number)
            for k in range(K):
                for h in range(2):
                    for part in range(2):
                        rows = pl.ds(8 * part * X + x, 8, stride=X)
                        O[h, k, rows, :] = new[k][h][8 * part : 8 * part + 8]

    traces = pltpu.make_async_remote_copy(
        O.at[:, :, pl.ds(0, X)], PR, p_sem.at[2], p_sem.at[3], device_id=partner, device_id_type=MESH
    )
    traces.start()
    sent(last)
    traces.wait()
    mine = jnp.where(fluid, 1.0 - THETA, THETA)
    other = jnp.where(fluid, THETA, 1.0 - THETA)
    for h in range(2):
        for k in range(K):
            IO[h, k] = mine * O[h, k, 0:X] + other * PR[h, k]


def write(a_ref, b_ref, o_ref, i_ref, sem):
    copies = [
        pltpu.make_async_copy(
            tile_ref.at[h], out_ref.at[..., pl.ds(h * LANES, LANES)], sem.at[n, h]
        )
        for n, (tile_ref, out_ref) in enumerate(((a_ref, o_ref), (b_ref, i_ref)))
        for h in range(2)
    ]
    for copy in copies:
        copy.start()
    for copy in copies:
        copy.wait()


def solution(mesh):
    nx, ny = mesh.shape["gx"], mesh.shape["gy"]

    def local(fields, source, reaction, velocity, coupling):
        _, _, L, X, Y = fields.shape
        spans = (3, 5)
        groups = len(spans)
        f32 = jnp.float32
        cells = L * X
        tiles, edges = pl.pallas_call(
            functools.partial(kernel, nx, ny, L, X, spans),
            out_shape=(
                pltpu.VMEM((2, K, cells, LANES), f32),
                pltpu.VMEM((2, K, X, LANES), f32),
            ),
            in_specs=[pl.BlockSpec(memory_space=pltpu.HBM)] * 5,
            out_specs=[pl.BlockSpec(memory_space=pltpu.VMEM)] * 2,
            scratch_shapes=[
                pltpu.VMEM((2, K, cells, LANES), f32),
                pltpu.VMEM((2, K, cells, LANES), f32),
                pltpu.VMEM((2, 2, cells, LANES), f32),
                pltpu.VMEM((SWEEPS, X + 2, 2, K, L, LANES), f32),
                pltpu.VMEM((2, K, X, L, LANES), f32),
                pltpu.VMEM((2, X, L, LANES), f32),
                pltpu.VMEM((2, K, X, L, LANES), f32),
                pltpu.VMEM((SWEEPS, groups, 2, 8, LANES), f32),
                pltpu.VMEM((SWEEPS, groups, 2, 8, LANES), f32),
                pltpu.VMEM((2, K, X, LANES), f32),
                pltpu.VMEM((2, K, X, LANES), f32),
                pltpu.VMEM((2, K, X, LANES), f32),
                pltpu.SemaphoreType.DMA((2,)),
                pltpu.SemaphoreType.DMA((2,)),
                pltpu.SemaphoreType.DMA((2, 2)),
                pltpu.SemaphoreType.DMA((SWEEPS, 2)),
                pltpu.SemaphoreType.DMA((SWEEPS, 2)),
                pltpu.SemaphoreType.DMA((SWEEPS, groups, 2)),
                pltpu.SemaphoreType.DMA((SWEEPS, groups, 2)),
                pltpu.SemaphoreType.DMA((4,)),
                pltpu.SMEM((K, 1, K), f32),
                pltpu.SemaphoreType.DMA,
            ],
            compiler_params=pltpu.CompilerParams(
                collective_id=0,
                has_side_effects=True,
                vmem_limit_bytes=60 * 1024 * 1024,
            ),
        )(
            fields.reshape(K, cells, Y),
            source.reshape(K, cells, Y),
            reaction.reshape(cells, Y),
            velocity.reshape(cells, Y),
            coupling.reshape(K, 1, K),
        )
        tiles, edges = (
            pltpu.with_memory_space_constraint(value, pltpu.VMEM) for value in (tiles, edges)
        )
        new, interface = pl.pallas_call(
            write,
            out_shape=(
                jax.ShapeDtypeStruct((K, cells, Y), f32),
                jax.ShapeDtypeStruct((K, X, Y), f32),
            ),
            in_specs=[pl.BlockSpec(memory_space=pltpu.VMEM)] * 2,
            out_specs=[pl.BlockSpec(memory_space=pltpu.HBM)] * 2,
            scratch_shapes=[pltpu.SemaphoreType.DMA((2, 2))],
        )(tiles, edges)
        return new.reshape(1, K, L, X, Y), interface[None]

    return jax.shard_map(
        local,
        mesh=mesh,
        in_specs=(
            P("side", None, None, "gx", "gy"),
            P("side", None, None, "gx", "gy"),
            P("side", None, "gx", "gy"),
            P("side", None, "gx", "gy"),
            P("side", None, None),
        ),
        out_specs=(P("side", None, None, "gx", "gy"), P("side", None, "gx", "gy")),
        check_vma=False,
    )
```

```python
import functools

import jax
import jax.numpy as jnp
from jax import lax
from jax.experimental import pallas as pl
from jax.experimental.pallas import tpu as pltpu
from jax.sharding import PartitionSpec as P

SWEEPS = 4
K = 3
OMEGA = 0.8
RATIO = 0.5
THETA = 0.7
LANES = 128
MESH = pl.DeviceIdType.MESH


def kernel(
    nx,
    ny,
    L,
    X,
    SPANS,
    f_ref,
    s_ref,
    r_ref,
    v_ref,
    c_ref,
    O,
    IO,
    F,
    S,
    RV,
    U,
    W,
    V1,
    SS,
    YO,
    YI,
    M,
    GH,
    PR,
    f_sem,
    s_sem,
    rv_sem,
    xs_sem,
    xr_sem,
    ys_sem,
    yr_sem,
    p_sem,
    C,
    c_sem,
):
    side = lax.axis_index("side")
    gx = lax.axis_index("gx")
    gy = lax.axis_index("gy")
    fluid = side == 0
    west = (side, lax.rem(gx + nx - 1, nx), gy)
    east = (side, lax.rem(gx + 1, nx), gy)
    south = (side, gx, gy - 1)
    north = (side, gx, gy + 1)
    partner = (1 - side, gx, gy)
    has_south = gy > 0
    has_north = gy < ny - 1
    groups = len(SPANS)

    barrier = pltpu.get_barrier_semaphore()

    def greet(device):
        pl.semaphore_signal(barrier, inc=1, device_id=device, device_id_type=MESH)

    greet(west)
    greet(east)
    greet(partner)
    pl.when(has_south)(lambda: greet(south))
    pl.when(has_north)(lambda: greet(north))

    def half(ref, h):
        return ref.at[..., pl.ds(h * LANES, LANES)]

    loads_f = [pltpu.make_async_copy(half(f_ref, h), F.at[h], f_sem.at[h]) for h in range(2)]
    loads_s = [pltpu.make_async_copy(half(s_ref, h), S.at[h], s_sem.at[h]) for h in range(2)]
    loads_rv = [
        pltpu.make_async_copy(half(ref, h), RV.at[n, h], rv_sem.at[n, h])
        for n, ref in enumerate((r_ref, v_ref))
        for h in range(2)
    ]
    load_c = pltpu.make_async_copy(c_ref, C, c_sem)
    for copy in loads_f + loads_rv + loads_s + [load_c]:
        copy.start()

    lane = lax.broadcasted_iota(jnp.int32, (8, LANES), 1)
    row = lax.broadcasted_iota(jnp.int32, (8, LANES), 0)
    place = lax.rem(lane + 1, LANES) // 2
    zero = jnp.zeros((8, LANES), jnp.float32)

    def x_copy(t, d):
        source, target = ((X, 0), (1, X + 1))[d]
        return pltpu.make_async_remote_copy(
            U.at[t, source],
            U.at[t, target],
            xs_sem.at[t, d],
            xr_sem.at[t, d],
            device_id=(east, west)[d],
            device_id_type=MESH,
        )

    def y_copy(t, g, d):
        return pltpu.make_async_remote_copy(
            YO.at[t, g],
            YI.at[t, g, d],
            ys_sem.at[t, g, d],
            yr_sem.at[t, g, d],
            device_id=(north, south)[d],
            device_id_type=MESH,
        )

    def x_both(t, step):
        for d in range(2):
            getattr(x_copy(t, d), step)()

    def y_start(t, g):
        pl.when(has_north)(lambda: y_copy(t, g, 0).start())
        pl.when(has_south)(lambda: y_copy(t, g, 1).start())

    def y_wait(t, g):
        pl.when(has_south)(lambda: y_copy(t, g, 0).wait_recv())
        pl.when(has_north)(lambda: y_copy(t, g, 1).wait_recv())

    def sent(t):
        x_both(t, "wait_send")
        for g in range(groups):
            pl.when(has_north)(lambda: y_copy(t, g, 0).wait_send())
            pl.when(has_south)(lambda: y_copy(t, g, 1).wait_send())

    def packed(packet, first, last, slot):
        both = jnp.where(lane == LANES - 1, last, first)
        return jnp.where(place == slot, pltpu.roll(both, 2 * slot, 1) if slot else both, packet)

    def arrived(t, g):
        return jnp.where(lax.rem(lane, 2) == 0, YI[t, g, 1], pltpu.roll(YI[t, g, 0], 2, 1))

    def slots(number, k):
        return [(number * K + k) * 2 + part for part in range(2)]

    def rows_of(g):
        start = sum(SPANS[:g])
        for n in range(SPANS[g]):
            yield start + n, 2 * n
            yield X - 1 - start - n, 2 * n + 1

    for copy in loads_f:
        copy.wait()

    for h in range(2):
        for k in range(K):
            layer0, layer1 = F[h, k, 0:X], F[h, k, X : 2 * X]
            M[h, k] = jnp.where(fluid, RATIO * (layer1 - layer0), layer0)

    for g in range(groups):
        packet = zero
        for x, number in rows_of(g):
            for k in range(K):
                for part, slot in enumerate(slots(number, k)):
                    rows = pl.ds(8 * part * X + x, 8, stride=X)
                    tiles = [F[h, k, rows, :] for h in range(2)]
                    for h in range(2):
                        U[0, x + 1, h, k, pl.ds(8 * part, 8)] = tiles[h]
                    packet = packed(packet, tiles[0], tiles[1], slot)
        YO[0, g] = packet

    greeted = 3 + has_south.astype(jnp.int32) + has_north.astype(jnp.int32)
    pl.semaphore_wait(barrier, greeted)

    for g in range(groups):
        y_start(0, g)
    x_both(0, "start")
    ghosts = pltpu.make_async_remote_copy(
        M, GH, p_sem.at[0], p_sem.at[1], device_id=partner, device_id_type=MESH
    )
    ghosts.start()

    def blank(d):
        for t in range(SWEEPS):
            for g in range(groups):
                YI[t, g, d] = zero

    pl.when(jnp.logical_not(has_south))(lambda: blank(0))
    pl.when(jnp.logical_not(has_north))(lambda: blank(1))

    for copy in loads_rv + loads_s + [load_c]:
        copy.wait()
    mix = [[C[k, 0, j] for j in range(K)] for k in range(K)]

    def weigh(x, carry):
        for h in range(2):
            for part in range(2):
                rows = pl.ds(8 * part * X + x, 8, stride=X)
                out = pl.ds(8 * part, 8)
                speed = RV[1, h, rows, :]
                diag = 6.0 + RV[0, h, rows, :] + speed
                V1[h, x, out] = 1.0 + speed
                for k in range(K):
                    W[h, k, x, out] = OMEGA / (diag + mix[k][k])
                    SS[h, k, x, out] = S[h, k, rows, :]
        return carry

    lax.fori_loop(0, X, weigh, 0)

    ghosts.wait()
    own = jnp.where(fluid, 0.0, 1.0)

    def relax(t, edges, x, number, parts=(0, 1)):
        tiles = [pl.ds(8 * part, 8) for part in range(2)]

        def state(x, h, k, part):
            return U[t, x + 1, h, k, tiles[part]]

        for part in parts:
            speeds = [V1[h, x, tiles[part]] for h in range(2)]
            center = [[state(x, h, k, part) for h in range(2)] for k in range(K)]
            for k in range(K):
                beyond = pltpu.roll(edges, LANES - 1 - 2 * slots(number, k)[part], 1)
                up = [pltpu.roll(center[k][h], 1, 1) for h in range(2)]
                down = [pltpu.roll(center[k][h], LANES - 1, 1) for h in range(2)]
                souths = (
                    jnp.where(lane == 0, beyond, up[0]),
                    jnp.where(lane == 0, up[0], up[1]),
                )
                norths = (
                    jnp.where(lane == LANES - 1, down[1], down[0]),
                    jnp.where(lane == LANES - 1, beyond, down[1]),
                )
                for h in range(2):
                    here = center[k][h]
                    beside = state(x, h, k, 1 - part)
                    if part == 0:
                        under = own * here + GH[h, k, pl.ds(x, 1), :]
                        over = pltpu.roll(beside, 7, 0)
                    else:
                        under = pltpu.roll(beside, 1, 0)
                        over = zero
                    below = jnp.where(row == 0, under, pltpu.roll(here, 1, 0))
                    above = jnp.where(row == 7, over, pltpu.roll(here, 7, 0))
                    total = SS[h, k, x, tiles[part]] + below + above
                    total = total + speeds[h] * state(x - 1, h, k, part) + state(x + 1, h, k, part)
                    total = total + souths[h] + norths[h]
                    for j in range(K):
                        if j != k:
                            total = total - mix[k][j] * center[j][h]
                    new = (1.0 - OMEGA) * here + W[h, k, x, tiles[part]] * total
                    yield k, h, part, new

    def advance(t, edges, x, number):
        for k, h, part, new in relax(t, edges, x, number):
            U[t + 1, x + 1, h, k, pl.ds(8 * part, 8)] = new

    def gather(t, g):
        packet = zero
        for x, number in rows_of(g):
            for k in range(K):
                for part, slot in enumerate(slots(number, k)):
                    first, last = (U[t, x + 1, h, k, pl.ds(8 * part, 8)] for h in range(2))
                    packet = packed(packet, first, last, slot)
        YO[t, g] = packet

    def sweep(t, carry):
        for g in range(groups):
            y_wait(t, g)
            if g == 0:
                x_both(t, "wait_recv")
            edges = arrived(t, g)
            for x, number in rows_of(g):
                advance(t, edges, x, number)
                if g == 0 and number == 1:
                    x_both(t + 1, "start")
            gather(t + 1, g)
            y_start(t + 1, g)
        sent(t)
        return carry

    lax.fori_loop(0, SWEEPS - 1, sweep, 0)

    traces = pltpu.make_async_remote_copy(
        O.at[:, :, pl.ds(0, X)], PR, p_sem.at[2], p_sem.at[3], device_id=partner, device_id_type=MESH
    )
    last = SWEEPS - 1
    x_both(last, "wait_recv")
    for part in range(2):
        for g in range(groups):
            if part == 0:
                y_wait(last, g)
            edges = arrived(last, g)
            for x, number in rows_of(g):
                for k, h, _, new in relax(last, edges, x, number, (part,)):
                    O[h, k, pl.ds(8 * part * X + x, 8, stride=X), :] = new
        if part == 0:
            traces.start()
    sent(last)
    traces.wait()
    mine = jnp.where(fluid, 1.0 - THETA, THETA)
    other = jnp.where(fluid, THETA, 1.0 - THETA)
    for h in range(2):
        for k in range(K):
            IO[h, k] = mine * O[h, k, 0:X] + other * PR[h, k]


def write(a_ref, b_ref, o_ref, i_ref, sem):
    copies = [
        pltpu.make_async_copy(
            tile_ref.at[h], out_ref.at[..., pl.ds(h * LANES, LANES)], sem.at[n, h]
        )
        for n, (tile_ref, out_ref) in enumerate(((a_ref, o_ref), (b_ref, i_ref)))
        for h in range(2)
    ]
    for copy in copies:
        copy.start()
    for copy in copies:
        copy.wait()


def solution(mesh):
    nx, ny = mesh.shape["gx"], mesh.shape["gy"]

    def local(fields, source, reaction, velocity, coupling):
        _, _, L, X, Y = fields.shape
        spans = (4, 4)
        groups = len(spans)
        f32 = jnp.float32
        cells = L * X
        tiles, edges = pl.pallas_call(
            functools.partial(kernel, nx, ny, L, X, spans),
            out_shape=(
                pltpu.VMEM((2, K, cells, LANES), f32),
                pltpu.VMEM((2, K, X, LANES), f32),
            ),
            in_specs=[pl.BlockSpec(memory_space=pltpu.HBM)] * 5,
            out_specs=[pl.BlockSpec(memory_space=pltpu.VMEM)] * 2,
            scratch_shapes=[
                pltpu.VMEM((2, K, cells, LANES), f32),
                pltpu.VMEM((2, K, cells, LANES), f32),
                pltpu.VMEM((2, 2, cells, LANES), f32),
                pltpu.VMEM((SWEEPS, X + 2, 2, K, L, LANES), f32),
                pltpu.VMEM((2, K, X, L, LANES), f32),
                pltpu.VMEM((2, X, L, LANES), f32),
                pltpu.VMEM((2, K, X, L, LANES), f32),
                pltpu.VMEM((SWEEPS, groups, 8, LANES), f32),
                pltpu.VMEM((SWEEPS, groups, 2, 8, LANES), f32),
                pltpu.VMEM((2, K, X, LANES), f32),
                pltpu.VMEM((2, K, X, LANES), f32),
                pltpu.VMEM((2, K, X, LANES), f32),
                pltpu.SemaphoreType.DMA((2,)),
                pltpu.SemaphoreType.DMA((2,)),
                pltpu.SemaphoreType.DMA((2, 2)),
                pltpu.SemaphoreType.DMA((SWEEPS, 2)),
                pltpu.SemaphoreType.DMA((SWEEPS, 2)),
                pltpu.SemaphoreType.DMA((SWEEPS, groups, 2)),
                pltpu.SemaphoreType.DMA((SWEEPS, groups, 2)),
                pltpu.SemaphoreType.DMA((4,)),
                pltpu.SMEM((K, 1, K), f32),
                pltpu.SemaphoreType.DMA,
            ],
            compiler_params=pltpu.CompilerParams(
                collective_id=0,
                has_side_effects=True,
                vmem_limit_bytes=60 * 1024 * 1024,
            ),
        )(
            fields.reshape(K, cells, Y),
            source.reshape(K, cells, Y),
            reaction.reshape(cells, Y),
            velocity.reshape(cells, Y),
            coupling.reshape(K, 1, K),
        )
        tiles, edges = (
            pltpu.with_memory_space_constraint(value, pltpu.VMEM) for value in (tiles, edges)
        )
        new, interface = pl.pallas_call(
            write,
            out_shape=(
                jax.ShapeDtypeStruct((K, cells, Y), f32),
                jax.ShapeDtypeStruct((K, X, Y), f32),
            ),
            in_specs=[pl.BlockSpec(memory_space=pltpu.VMEM)] * 2,
            out_specs=[pl.BlockSpec(memory_space=pltpu.HBM)] * 2,
            scratch_shapes=[pltpu.SemaphoreType.DMA((2, 2))],
        )(tiles, edges)
        return new.reshape(1, K, L, X, Y), interface[None]

    return jax.shard_map(
        local,
        mesh=mesh,
        in_specs=(
            P("side", None, None, "gx", "gy"),
            P("side", None, None, "gx", "gy"),
            P("side", None, "gx", "gy"),
            P("side", None, "gx", "gy"),
            P("side", None, None),
        ),
        out_specs=(P("side", None, None, "gx", "gy"), P("side", None, "gx", "gy")),
        check_vma=False,
    )
```

```python
import functools

import jax
import jax.numpy as jnp
from jax import lax
from jax.experimental import pallas as pl
from jax.experimental.pallas import tpu as pltpu
from jax.sharding import PartitionSpec as P

SWEEPS = 4
K = 3
OMEGA = 0.8
RATIO = 0.5
THETA = 0.7
LANES = 128
MESH = pl.DeviceIdType.MESH


def kernel(
    nx,
    ny,
    L,
    X,
    f_ref,
    s_ref,
    r_ref,
    v_ref,
    c_ref,
    O,
    IO,
    F,
    S,
    RV,
    U,
    W,
    V1,
    SS,
    YO,
    YI,
    M,
    GH,
    PR,
    f_sem,
    s_sem,
    rv_sem,
    xs_sem,
    xr_sem,
    ys_sem,
    yr_sem,
    p_sem,
    C,
    c_sem,
):
    side = lax.axis_index("side")
    gx = lax.axis_index("gx")
    gy = lax.axis_index("gy")
    fluid = side == 0
    west = (side, lax.rem(gx + nx - 1, nx), gy)
    east = (side, lax.rem(gx + 1, nx), gy)
    south = (side, gx, gy - 1)
    north = (side, gx, gy + 1)
    partner = (1 - side, gx, gy)
    has_south = gy > 0
    has_north = gy < ny - 1

    barrier = pltpu.get_barrier_semaphore()

    def greet(device):
        pl.semaphore_signal(barrier, inc=1, device_id=device, device_id_type=MESH)

    greet(west)
    greet(east)
    greet(partner)
    pl.when(has_south)(lambda: greet(south))
    pl.when(has_north)(lambda: greet(north))

    def half(ref, h):
        return ref.at[..., pl.ds(h * LANES, LANES)]

    loads_f = [pltpu.make_async_copy(half(f_ref, h), F.at[h], f_sem.at[h]) for h in range(2)]
    loads_s = [pltpu.make_async_copy(half(s_ref, h), S.at[h], s_sem.at[h]) for h in range(2)]
    loads_rv = [
        pltpu.make_async_copy(half(ref, h), RV.at[n, h], rv_sem.at[n, h])
        for n, ref in enumerate((r_ref, v_ref))
        for h in range(2)
    ]
    load_c = pltpu.make_async_copy(c_ref, C, c_sem)
    for copy in loads_f + loads_rv + loads_s + [load_c]:
        copy.start()

    lane = lax.broadcasted_iota(jnp.int32, (8, LANES), 1)
    row = lax.broadcasted_iota(jnp.int32, (8, LANES), 0)
    zero = jnp.zeros((8, LANES), jnp.float32)

    def x_copy(t, d, h):
        source, target = ((X, 0), (1, X + 1))[d]
        return pltpu.make_async_remote_copy(
            U.at[t, source, h],
            U.at[t, target, h],
            xs_sem.at[t, d, h],
            xr_sem.at[t, d, h],
            device_id=(east, west)[d],
            device_id_type=MESH,
        )

    def y_copy(t, g, d):
        return pltpu.make_async_remote_copy(
            YO.at[t, g, d],
            YI.at[t, g, d],
            ys_sem.at[t, g, d],
            yr_sem.at[t, g, d],
            device_id=(north, south)[d],
            device_id_type=MESH,
        )

    quarters = [(g, h) for g in range(2) for h in range(2)]

    def y_start(t, g, h):
        pl.when((has_south, has_north)[h])(lambda: y_copy(t, g, 1 - h).start())

    def y_sent(t, g, h):
        pl.when((has_south, has_north)[h])(lambda: y_copy(t, g, 1 - h).wait_send())

    def arrive(t, g, h):
        pl.when((has_south, has_north)[h])(lambda: y_copy(t, g, h).wait_recv())
        x_copy(t, 1 - g, h).wait_recv()

    def sent(t):
        for g, h in quarters:
            x_copy(t, g, h).wait_send()
            y_sent(t, g, h)

    def packed(packet, tile, h, slot):
        shift = slot + h
        moved = pltpu.roll(tile, shift, 1) if shift else tile
        return jnp.where(lane == slot, moved, packet)

    def unpacked(packet, h, slot):
        shift = (h * (LANES - 1) - slot) % LANES
        return pltpu.roll(packet, shift, 1) if shift else packet

    def slots(number, k):
        return [(number * K + k) * 2 + part for part in range(2)]

    def rows_of(g):
        return [(n if g else X - 1 - n, n) for n in range(X // 2)]

    for copy in loads_f:
        copy.wait()

    for h in range(2):
        for k in range(K):
            layer0, layer1 = F[h, k, 0:X], F[h, k, X : 2 * X]
            M[h, k] = jnp.where(fluid, RATIO * (layer1 - layer0), layer0)

    for g, h in quarters:
        packet = zero
        for x, number in rows_of(g):
            for k in range(K):
                for part, slot in enumerate(slots(number, k)):
                    tile = F[h, k, pl.ds(8 * part * X + x, 8, stride=X), :]
                    U[0, x + 1, h, k, pl.ds(8 * part, 8)] = tile
                    packet = packed(packet, tile, h, slot)
        YO[0, g, 1 - h] = packet

    greeted = 3 + has_south.astype(jnp.int32) + has_north.astype(jnp.int32)
    pl.semaphore_wait(barrier, greeted)

    for g, h in quarters:
        y_start(0, g, h)
    for g, h in quarters:
        x_copy(0, g, h).start()
    ghosts = pltpu.make_async_remote_copy(
        M, GH, p_sem.at[0], p_sem.at[1], device_id=partner, device_id_type=MESH
    )
    ghosts.start()

    def blank(d):
        for t in range(SWEEPS):
            for g in range(2):
                YI[t, g, d] = zero

    pl.when(jnp.logical_not(has_south))(lambda: blank(0))
    pl.when(jnp.logical_not(has_north))(lambda: blank(1))

    for copy in loads_rv + loads_s + [load_c]:
        copy.wait()
    mix = [[C[k, 0, j] for j in range(K)] for k in range(K)]

    def weigh(x, carry):
        for h in range(2):
            for part in range(2):
                rows = pl.ds(8 * part * X + x, 8, stride=X)
                out = pl.ds(8 * part, 8)
                speed = RV[1, h, rows, :]
                diag = 6.0 + RV[0, h, rows, :] + speed
                V1[h, x, out] = 1.0 + speed
                for k in range(K):
                    W[h, k, x, out] = OMEGA / (diag + mix[k][k])
                    SS[h, k, x, out] = S[h, k, rows, :]
        return carry

    lax.fori_loop(0, X, weigh, 0)

    ghosts.wait()
    own = jnp.where(fluid, 0.0, 1.0)

    def relax(t, packet, x, number, h, parts=(0, 1)):
        tiles = [pl.ds(8 * part, 8) for part in range(2)]
        outer, inner = ((0, LANES - 1), (LANES - 1, 0))[h]
        away, back = ((1, LANES - 1), (LANES - 1, 1))[h]

        def state(x, h, k, part):
            return U[t, x + 1, h, k, tiles[part]]

        for part in parts:
            speed = V1[h, x, tiles[part]]
            center = [state(x, h, k, part) for k in range(K)]
            for k in range(K):
                here = center[k]
                beyond = unpacked(packet, h, slots(number, k)[part])
                outwards = jnp.where(lane == outer, beyond, pltpu.roll(here, away, 1))
                across = jnp.where(lane == outer, state(x, 1 - h, k, part), here)
                inwards = pltpu.roll(across, back, 1)
                beside = state(x, h, k, 1 - part)
                if part == 0:
                    under = own * here + GH[h, k, pl.ds(x, 1), :]
                    over = pltpu.roll(beside, 7, 0)
                else:
                    under = pltpu.roll(beside, 1, 0)
                    over = zero
                below = jnp.where(row == 0, under, pltpu.roll(here, 1, 0))
                above = jnp.where(row == 7, over, pltpu.roll(here, 7, 0))
                total = SS[h, k, x, tiles[part]] + below + above
                total = total + speed * state(x - 1, h, k, part) + state(x + 1, h, k, part)
                total = total + outwards + inwards
                for j in range(K):
                    if j != k:
                        total = total - mix[k][j] * center[j]
                yield k, part, (1.0 - OMEGA) * here + W[h, k, x, tiles[part]] * total

    def gather(t, g, h):
        packet = zero
        for x, number in rows_of(g):
            for k in range(K):
                for part, slot in enumerate(slots(number, k)):
                    packet = packed(packet, U[t, x + 1, h, k, pl.ds(8 * part, 8)], h, slot)
        YO[t, g, 1 - h] = packet

    def sweep(t, carry):
        for g, h in quarters:
            arrive(t, g, h)
            packet = YI[t, g, h]
            for x, number in rows_of(g):
                for k, part, new in relax(t, packet, x, number, h):
                    U[t + 1, x + 1, h, k, pl.ds(8 * part, 8)] = new
                if number == 0:
                    x_copy(t + 1, g, h).start()
            gather(t + 1, g, h)
            y_start(t + 1, g, h)
        sent(t)
        return carry

    lax.fori_loop(0, SWEEPS - 1, sweep, 0)

    traces = pltpu.make_async_remote_copy(
        O.at[:, :, pl.ds(0, X)], PR, p_sem.at[2], p_sem.at[3], device_id=partner, device_id_type=MESH
    )
    last = SWEEPS - 1
    for part in range(2):
        for g, h in quarters:
            if part == 0:
                arrive(last, g, h)
            packet = YI[last, g, h]
            for x, number in rows_of(g):
                for k, _, new in relax(last, packet, x, number, h, (part,)):
                    O[h, k, pl.ds(8 * part * X + x, 8, stride=X), :] = new
        if part == 0:
            traces.start()
    sent(last)
    traces.wait()
    mine = jnp.where(fluid, 1.0 - THETA, THETA)
    other = jnp.where(fluid, THETA, 1.0 - THETA)
    for h in range(2):
        for k in range(K):
            IO[h, k] = mine * O[h, k, 0:X] + other * PR[h, k]


def write(a_ref, b_ref, o_ref, i_ref, sem):
    copies = [
        pltpu.make_async_copy(
            tile_ref.at[h], out_ref.at[..., pl.ds(h * LANES, LANES)], sem.at[n, h]
        )
        for n, (tile_ref, out_ref) in enumerate(((a_ref, o_ref), (b_ref, i_ref)))
        for h in range(2)
    ]
    for copy in copies:
        copy.start()
    for copy in copies:
        copy.wait()


def solution(mesh):
    nx, ny = mesh.shape["gx"], mesh.shape["gy"]

    def local(fields, source, reaction, velocity, coupling):
        _, _, L, X, Y = fields.shape
        groups = 2
        f32 = jnp.float32
        cells = L * X
        tiles, edges = pl.pallas_call(
            functools.partial(kernel, nx, ny, L, X),
            out_shape=(
                pltpu.VMEM((2, K, cells, LANES), f32),
                pltpu.VMEM((2, K, X, LANES), f32),
            ),
            in_specs=[pl.BlockSpec(memory_space=pltpu.HBM)] * 5,
            out_specs=[pl.BlockSpec(memory_space=pltpu.VMEM)] * 2,
            scratch_shapes=[
                pltpu.VMEM((2, K, cells, LANES), f32),
                pltpu.VMEM((2, K, cells, LANES), f32),
                pltpu.VMEM((2, 2, cells, LANES), f32),
                pltpu.VMEM((SWEEPS, X + 2, 2, K, L, LANES), f32),
                pltpu.VMEM((2, K, X, L, LANES), f32),
                pltpu.VMEM((2, X, L, LANES), f32),
                pltpu.VMEM((2, K, X, L, LANES), f32),
                pltpu.VMEM((SWEEPS, groups, 2, 8, LANES), f32),
                pltpu.VMEM((SWEEPS, groups, 2, 8, LANES), f32),
                pltpu.VMEM((2, K, X, LANES), f32),
                pltpu.VMEM((2, K, X, LANES), f32),
                pltpu.VMEM((2, K, X, LANES), f32),
                pltpu.SemaphoreType.DMA((2,)),
                pltpu.SemaphoreType.DMA((2,)),
                pltpu.SemaphoreType.DMA((2, 2)),
                pltpu.SemaphoreType.DMA((SWEEPS, 2, 2)),
                pltpu.SemaphoreType.DMA((SWEEPS, 2, 2)),
                pltpu.SemaphoreType.DMA((SWEEPS, groups, 2)),
                pltpu.SemaphoreType.DMA((SWEEPS, groups, 2)),
                pltpu.SemaphoreType.DMA((4,)),
                pltpu.SMEM((K, 1, K), f32),
                pltpu.SemaphoreType.DMA,
            ],
            compiler_params=pltpu.CompilerParams(
                collective_id=0,
                has_side_effects=True,
                vmem_limit_bytes=60 * 1024 * 1024,
            ),
        )(
            fields.reshape(K, cells, Y),
            source.reshape(K, cells, Y),
            reaction.reshape(cells, Y),
            velocity.reshape(cells, Y),
            coupling.reshape(K, 1, K),
        )
        tiles, edges = (
            pltpu.with_memory_space_constraint(value, pltpu.VMEM) for value in (tiles, edges)
        )
        new, interface = pl.pallas_call(
            write,
            out_shape=(
                jax.ShapeDtypeStruct((K, cells, Y), f32),
                jax.ShapeDtypeStruct((K, X, Y), f32),
            ),
            in_specs=[pl.BlockSpec(memory_space=pltpu.VMEM)] * 2,
            out_specs=[pl.BlockSpec(memory_space=pltpu.HBM)] * 2,
            scratch_shapes=[pltpu.SemaphoreType.DMA((2, 2))],
        )(tiles, edges)
        return new.reshape(1, K, L, X, Y), interface[None]

    return jax.shard_map(
        local,
        mesh=mesh,
        in_specs=(
            P("side", None, None, "gx", "gy"),
            P("side", None, None, "gx", "gy"),
            P("side", None, "gx", "gy"),
            P("side", None, "gx", "gy"),
            P("side", None, None),
        ),
        out_specs=(P("side", None, None, "gx", "gy"), P("side", None, "gx", "gy")),
        check_vma=False,
    )
```

```python
import functools

import jax
import jax.numpy as jnp
from jax import lax
from jax.experimental import pallas as pl
from jax.experimental.pallas import tpu as pltpu
from jax.sharding import PartitionSpec as P

SWEEPS = 4
K = 3
OMEGA = 0.8
RATIO = 0.5
THETA = 0.7
LANES = 128
MESH = pl.DeviceIdType.MESH


def kernel(
    nx,
    ny,
    L,
    X,
    f_ref,
    s_ref,
    r_ref,
    v_ref,
    c_ref,
    O,
    IO,
    F,
    S,
    RV,
    U,
    W,
    V1,
    SS,
    YO,
    YI,
    M,
    GH,
    PR,
    f_sem,
    s_sem,
    rv_sem,
    xs_sem,
    xr_sem,
    ys_sem,
    yr_sem,
    p_sem,
    ts_sem,
    tr_sem,
    C,
    c_sem,
):
    side = lax.axis_index("side")
    gx = lax.axis_index("gx")
    gy = lax.axis_index("gy")
    fluid = side == 0
    west = (side, lax.rem(gx + nx - 1, nx), gy)
    east = (side, lax.rem(gx + 1, nx), gy)
    south = (side, gx, gy - 1)
    north = (side, gx, gy + 1)
    partner = (1 - side, gx, gy)
    has_south = gy > 0
    has_north = gy < ny - 1

    barrier = pltpu.get_barrier_semaphore()

    def greet(device):
        pl.semaphore_signal(barrier, inc=1, device_id=device, device_id_type=MESH)

    greet(west)
    greet(east)
    greet(partner)
    pl.when(has_south)(lambda: greet(south))
    pl.when(has_north)(lambda: greet(north))

    def half(ref, h):
        return ref.at[..., pl.ds(h * LANES, LANES)]

    loads_f = [pltpu.make_async_copy(half(f_ref, h), F.at[h], f_sem.at[h]) for h in range(2)]
    loads_s = [pltpu.make_async_copy(half(s_ref, h), S.at[h], s_sem.at[h]) for h in range(2)]
    loads_rv = [
        pltpu.make_async_copy(half(ref, h), RV.at[n, h], rv_sem.at[n, h])
        for n, ref in enumerate((r_ref, v_ref))
        for h in range(2)
    ]
    load_c = pltpu.make_async_copy(c_ref, C, c_sem)
    for copy in loads_f + loads_rv + loads_s + [load_c]:
        copy.start()

    lane = lax.broadcasted_iota(jnp.int32, (8, LANES), 1)
    zero = jnp.zeros((8, LANES), jnp.float32)

    def x_copy(t, d, h):
        source, target = ((X, 0), (1, X + 1))[d]
        return pltpu.make_async_remote_copy(
            U.at[t, source, h, :, pl.ds(8, L)],
            U.at[t, target, h, :, pl.ds(8, L)],
            xs_sem.at[t, d, h],
            xr_sem.at[t, d, h],
            device_id=(east, west)[d],
            device_id_type=MESH,
        )

    def y_copy(t, g, d):
        return pltpu.make_async_remote_copy(
            YO.at[t, g, d],
            YI.at[t, g, d],
            ys_sem.at[t, g, d],
            yr_sem.at[t, g, d],
            device_id=(north, south)[d],
            device_id_type=MESH,
        )

    quarters = [(g, h) for g in range(2) for h in range(2)]

    def y_start(t, g, h):
        pl.when((has_south, has_north)[h])(lambda: y_copy(t, g, 1 - h).start())

    def y_sent(t, g, h):
        pl.when((has_south, has_north)[h])(lambda: y_copy(t, g, 1 - h).wait_send())

    def arrive(t, g, h):
        pl.when((has_south, has_north)[h])(lambda: y_copy(t, g, h).wait_recv())
        x_copy(t, 1 - g, h).wait_recv()

    def sent(t):
        for g, h in quarters:
            x_copy(t, g, h).wait_send()
            y_sent(t, g, h)

    def packed(packet, tile, h, slot):
        shift = slot + h
        moved = pltpu.roll(tile, shift, 1) if shift else tile
        return jnp.where(lane == slot, moved, packet)

    def unpacked(packet, h, slot):
        shift = (h * (LANES - 1) - slot) % LANES
        return pltpu.roll(packet, shift, 1) if shift else packet

    def slots(number, k):
        return [(number * K + k) * 2 + part for part in range(2)]

    def rows_of(g):
        return [(n if g else X - 1 - n, n) for n in range(X // 2)]

    for copy in loads_f:
        copy.wait()

    for h in range(2):
        for k in range(K):
            layer0, layer1 = F[h, k, 0:X], F[h, k, X : 2 * X]
            M[h, k] = jnp.where(fluid, RATIO * (layer1 - layer0), layer0)

    for g, h in quarters:
        packet = zero
        for x, number in rows_of(g):
            for k in range(K):
                for part, slot in enumerate(slots(number, k)):
                    tile = F[h, k, pl.ds(8 * part * X + x, 8, stride=X), :]
                    U[0, x + 1, h, k, pl.ds(8 + 8 * part, 8)] = tile
                    packet = packed(packet, tile, h, slot)
        YO[0, g, 1 - h] = packet

    greeted = 3 + has_south.astype(jnp.int32) + has_north.astype(jnp.int32)
    pl.semaphore_wait(barrier, greeted)

    for g, h in quarters:
        y_start(0, g, h)
    for g, h in quarters:
        x_copy(0, g, h).start()
    ghosts = pltpu.make_async_remote_copy(
        M, GH, p_sem.at[0], p_sem.at[1], device_id=partner, device_id_type=MESH
    )
    ghosts.start()

    def blank(d):
        for t in range(SWEEPS):
            for g in range(2):
                YI[t, g, d] = zero

    pl.when(jnp.logical_not(has_south))(lambda: blank(0))
    pl.when(jnp.logical_not(has_north))(lambda: blank(1))

    for copy in loads_rv + loads_s + [load_c]:
        copy.wait()
    mix = [[C[k, 0, j] for j in range(K)] for k in range(K)]

    def weigh(x, carry):
        for h in range(2):
            for part in range(2):
                rows = pl.ds(8 * part * X + x, 8, stride=X)
                out = pl.ds(8 * part, 8)
                speed = RV[1, h, rows, :]
                diag = 6.0 + RV[0, h, rows, :] + speed
                V1[h, x, out] = 1.0 + speed
                for k in range(K):
                    W[h, k, x, out] = OMEGA / (diag + mix[k][k])
                    SS[h, k, x, out] = S[h, k, rows, :]
        return carry

    lax.fori_loop(0, X, weigh, 0)

    ghosts.wait()
    own = jnp.where(fluid, 0.0, 1.0)

    def ghost(h, k, x, layer):
        return own * layer + GH[h, k, pl.ds(x, 1), :]

    def frame(x, carry):
        for h in range(2):
            for k in range(K):
                for t in range(SWEEPS):
                    U[t, x + 1, h, k, pl.ds(8 + L, 8)] = zero
                U[0, x + 1, h, k, 7:8] = ghost(h, k, x, U[0, x + 1, h, k, 8:9])
        return carry

    lax.fori_loop(0, X, frame, 0)

    def relax(t, packet, x, number, h, parts=(0, 1)):
        tiles = [pl.ds(8 * part, 8) for part in range(2)]
        outer, inner = ((0, LANES - 1), (LANES - 1, 0))[h]
        away, back = ((1, LANES - 1), (LANES - 1, 1))[h]

        def state(x, h, k, part, up=0):
            return U[t, x + 1, h, k, pl.ds(8 + 8 * part + up, 8)]

        for part in parts:
            speed = V1[h, x, tiles[part]]
            center = [state(x, h, k, part) for k in range(K)]
            for k in range(K):
                here = center[k]
                beyond = unpacked(packet, h, slots(number, k)[part])
                outwards = jnp.where(lane == outer, beyond, pltpu.roll(here, away, 1))
                across = jnp.where(lane == outer, state(x, 1 - h, k, part), here)
                inwards = pltpu.roll(across, back, 1)
                total = SS[h, k, x, tiles[part]] + state(x, h, k, part, -1) + state(x, h, k, part, 1)
                total = total + speed * state(x - 1, h, k, part) + state(x + 1, h, k, part)
                total = total + outwards + inwards
                for j in range(K):
                    if j != k:
                        total = total - mix[k][j] * center[j]
                yield k, part, (1.0 - OMEGA) * here + W[h, k, x, tiles[part]] * total

    def gather(t, g, h):
        packet = zero
        for x, number in rows_of(g):
            for k in range(K):
                for part, slot in enumerate(slots(number, k)):
                    packet = packed(packet, U[t, x + 1, h, k, pl.ds(8 + 8 * part, 8)], h, slot)
        YO[t, g, 1 - h] = packet

    def sweep(t, carry):
        for g, h in quarters:
            arrive(t, g, h)
            packet = YI[t, g, h]
            for x, number in rows_of(g):
                for k, part, new in relax(t, packet, x, number, h):
                    U[t + 1, x + 1, h, k, pl.ds(8 + 8 * part, 8)] = new
                    if part == 0:
                        U[t + 1, x + 1, h, k, 7:8] = ghost(h, k, x, new[0:1])
            gather(t + 1, g, h)
            y_start(t + 1, g, h)
            x_copy(t + 1, g, h).start()
        sent(t)
        return carry

    lax.fori_loop(0, SWEEPS - 1, sweep, 0)

    last = SWEEPS - 1
    half_rows = X // 2

    def trace(g, h):
        rows = pl.ds((1 - g) * half_rows, half_rows)
        return pltpu.make_async_remote_copy(
            O.at[h, :, rows],
            PR.at[h, :, rows],
            ts_sem.at[g, h],
            tr_sem.at[g, h],
            device_id=partner,
            device_id_type=MESH,
        )

    for g, h in quarters:
        arrive(last, g, h)
        packet = YI[last, g, h]
        for part in range(2):
            for x, number in rows_of(g):
                for k, _, new in relax(last, packet, x, number, h, (part,)):
                    O[h, k, pl.ds(8 * part * X + x, 8, stride=X), :] = new
            if part == 0:
                trace(g, h).start()
    sent(last)
    mine = jnp.where(fluid, 1.0 - THETA, THETA)
    other = jnp.where(fluid, THETA, 1.0 - THETA)
    for g, h in quarters:
        trace(g, h).wait()
        rows = pl.ds((1 - g) * half_rows, half_rows)
        for k in range(K):
            IO[h, k, rows] = mine * O[h, k, rows] + other * PR[h, k, rows]


def write(a_ref, b_ref, o_ref, i_ref, sem):
    copies = [
        pltpu.make_async_copy(
            tile_ref.at[h], out_ref.at[..., pl.ds(h * LANES, LANES)], sem.at[n, h]
        )
        for n, (tile_ref, out_ref) in enumerate(((a_ref, o_ref), (b_ref, i_ref)))
        for h in range(2)
    ]
    for copy in copies:
        copy.start()
    for copy in copies:
        copy.wait()


def solution(mesh):
    nx, ny = mesh.shape["gx"], mesh.shape["gy"]

    def local(fields, source, reaction, velocity, coupling):
        _, _, L, X, Y = fields.shape
        groups = 2
        f32 = jnp.float32
        cells = L * X
        tiles, edges = pl.pallas_call(
            functools.partial(kernel, nx, ny, L, X),
            out_shape=(
                pltpu.VMEM((2, K, cells, LANES), f32),
                pltpu.VMEM((2, K, X, LANES), f32),
            ),
            in_specs=[pl.BlockSpec(memory_space=pltpu.HBM)] * 5,
            out_specs=[pl.BlockSpec(memory_space=pltpu.VMEM)] * 2,
            scratch_shapes=[
                pltpu.VMEM((2, K, cells, LANES), f32),
                pltpu.VMEM((2, K, cells, LANES), f32),
                pltpu.VMEM((2, 2, cells, LANES), f32),
                pltpu.VMEM((SWEEPS, X + 2, 2, K, L + 16, LANES), f32),
                pltpu.VMEM((2, K, X, L, LANES), f32),
                pltpu.VMEM((2, X, L, LANES), f32),
                pltpu.VMEM((2, K, X, L, LANES), f32),
                pltpu.VMEM((SWEEPS, groups, 2, 8, LANES), f32),
                pltpu.VMEM((SWEEPS, groups, 2, 8, LANES), f32),
                pltpu.VMEM((2, K, X, LANES), f32),
                pltpu.VMEM((2, K, X, LANES), f32),
                pltpu.VMEM((2, K, X, LANES), f32),
                pltpu.SemaphoreType.DMA((2,)),
                pltpu.SemaphoreType.DMA((2,)),
                pltpu.SemaphoreType.DMA((2, 2)),
                pltpu.SemaphoreType.DMA((SWEEPS, 2, 2)),
                pltpu.SemaphoreType.DMA((SWEEPS, 2, 2)),
                pltpu.SemaphoreType.DMA((SWEEPS, groups, 2)),
                pltpu.SemaphoreType.DMA((SWEEPS, groups, 2)),
                pltpu.SemaphoreType.DMA((2,)),
                pltpu.SemaphoreType.DMA((2, 2)),
                pltpu.SemaphoreType.DMA((2, 2)),
                pltpu.SMEM((K, 1, K), f32),
                pltpu.SemaphoreType.DMA,
            ],
            compiler_params=pltpu.CompilerParams(
                collective_id=0,
                has_side_effects=True,
                vmem_limit_bytes=60 * 1024 * 1024,
            ),
        )(
            fields.reshape(K, cells, Y),
            source.reshape(K, cells, Y),
            reaction.reshape(cells, Y),
            velocity.reshape(cells, Y),
            coupling.reshape(K, 1, K),
        )
        tiles, edges = (
            pltpu.with_memory_space_constraint(value, pltpu.VMEM) for value in (tiles, edges)
        )
        new, interface = pl.pallas_call(
            write,
            out_shape=(
                jax.ShapeDtypeStruct((K, cells, Y), f32),
                jax.ShapeDtypeStruct((K, X, Y), f32),
            ),
            in_specs=[pl.BlockSpec(memory_space=pltpu.VMEM)] * 2,
            out_specs=[pl.BlockSpec(memory_space=pltpu.HBM)] * 2,
            scratch_shapes=[pltpu.SemaphoreType.DMA((2, 2))],
        )(tiles, edges)
        return new.reshape(1, K, L, X, Y), interface[None]

    return jax.shard_map(
        local,
        mesh=mesh,
        in_specs=(
            P("side", None, None, "gx", "gy"),
            P("side", None, None, "gx", "gy"),
            P("side", None, "gx", "gy"),
            P("side", None, "gx", "gy"),
            P("side", None, None),
        ),
        out_specs=(P("side", None, None, "gx", "gy"), P("side", None, "gx", "gy")),
        check_vma=False,
    )
```

```python
import functools

import jax
import jax.numpy as jnp
from jax import lax
from jax.experimental import pallas as pl
from jax.experimental.pallas import tpu as pltpu
from jax.sharding import PartitionSpec as P

SWEEPS = 4
K = 3
OMEGA = 0.8
RATIO = 0.5
THETA = 0.7
LANES = 128
MESH = pl.DeviceIdType.MESH


def kernel(
    nx,
    ny,
    L,
    X,
    f_ref,
    s_ref,
    r_ref,
    v_ref,
    c_ref,
    O,
    IO,
    F,
    S,
    RV,
    U,
    W,
    V1,
    SS,
    YO,
    YI,
    M,
    GH,
    PR,
    f_sem,
    s_sem,
    rv_sem,
    xs_sem,
    xr_sem,
    ys_sem,
    yr_sem,
    p_sem,
    ts_sem,
    tr_sem,
    C,
    c_sem,
    WP,
):
    side = lax.axis_index("side")
    gx = lax.axis_index("gx")
    gy = lax.axis_index("gy")
    fluid = side == 0
    west = (side, lax.rem(gx + nx - 1, nx), gy)
    east = (side, lax.rem(gx + 1, nx), gy)
    south = (side, gx, gy - 1)
    north = (side, gx, gy + 1)
    partner = (1 - side, gx, gy)
    has_south = gy > 0
    has_north = gy < ny - 1

    barrier = pltpu.get_barrier_semaphore()

    def greet(device):
        pl.semaphore_signal(barrier, inc=1, device_id=device, device_id_type=MESH)

    greet(west)
    greet(east)
    greet(partner)
    pl.when(has_south)(lambda: greet(south))
    pl.when(has_north)(lambda: greet(north))

    def half(ref, h):
        return ref.at[..., pl.ds(h * LANES, LANES)]

    loads_f = [pltpu.make_async_copy(half(f_ref, h), F.at[h], f_sem.at[h]) for h in range(2)]
    loads_s = [pltpu.make_async_copy(half(s_ref, h), S.at[h], s_sem.at[h]) for h in range(2)]
    loads_rv = [
        pltpu.make_async_copy(half(ref, h), RV.at[n, h], rv_sem.at[n, h])
        for n, ref in enumerate((r_ref, v_ref))
        for h in range(2)
    ]
    load_c = pltpu.make_async_copy(c_ref, C, c_sem)
    for copy in loads_f + loads_rv + loads_s + [load_c]:
        copy.start()

    lane = lax.broadcasted_iota(jnp.int32, (8, LANES), 1)
    zero = jnp.zeros((8, LANES), jnp.float32)

    def x_copy(t, d, h):
        source, target = ((X, 0), (1, X + 1))[d]
        return pltpu.make_async_remote_copy(
            U.at[t, source, h, :, pl.ds(8, L)],
            U.at[t, target, h, :, pl.ds(8, L)],
            xs_sem.at[t, d, h],
            xr_sem.at[t, d, h],
            device_id=(east, west)[d],
            device_id_type=MESH,
        )

    def y_copy(t, g, d):
        return pltpu.make_async_remote_copy(
            YO.at[t, g, d],
            YI.at[t, g, d],
            ys_sem.at[t, g, d],
            yr_sem.at[t, g, d],
            device_id=(north, south)[d],
            device_id_type=MESH,
        )

    quarters = [(g, h) for g in range(2) for h in range(2)]

    def y_start(t, g, h):
        pl.when((has_south, has_north)[h])(lambda: y_copy(t, g, 1 - h).start())

    def y_sent(t, g, h):
        pl.when((has_south, has_north)[h])(lambda: y_copy(t, g, 1 - h).wait_send())

    def y_wait(t, g, h):
        pl.when((has_south, has_north)[h])(lambda: y_copy(t, g, h).wait_recv())

    def sent(t):
        for g, h in quarters:
            x_copy(t, g, h).wait_send()
            y_sent(t, g, h)

    def packed(packet, tile, h, slot):
        shift = slot + h
        moved = pltpu.roll(tile, shift, 1) if shift else tile
        return jnp.where(lane == slot, moved, packet)

    def unpacked(packet, h, slot):
        shift = (h * (LANES - 1) - slot) % LANES
        return pltpu.roll(packet, shift, 1) if shift else packet

    def slots(number, k):
        return [(number * K + k) * 2 + part for part in range(2)]

    def rows_of(g):
        return [(n if g else X - 1 - n, n) for n in range(X // 2)]

    for copy in loads_f:
        copy.wait()

    for h in range(2):
        for k in range(K):
            layer0, layer1 = F[h, k, 0:X], F[h, k, X : 2 * X]
            M[h, k] = jnp.where(fluid, RATIO * (layer1 - layer0), layer0)

    for g, h in quarters:
        packet = zero
        for x, number in rows_of(g):
            for k in range(K):
                for part, slot in enumerate(slots(number, k)):
                    tile = F[h, k, pl.ds(8 * part * X + x, 8, stride=X), :]
                    U[0, x + 1, h, k, pl.ds(8 + 8 * part, 8)] = tile
                    packet = packed(packet, tile, h, slot)
        YO[0, g, 1 - h] = packet

    greeted = 3 + has_south.astype(jnp.int32) + has_north.astype(jnp.int32)
    pl.semaphore_wait(barrier, greeted)

    for g, h in quarters:
        y_start(0, g, h)
    for g, h in quarters:
        x_copy(0, g, h).start()
    ghosts = pltpu.make_async_remote_copy(
        M, GH, p_sem.at[0], p_sem.at[1], device_id=partner, device_id_type=MESH
    )
    ghosts.start()

    def blank(d):
        for t in range(SWEEPS):
            for g in range(2):
                YI[t, g, d] = zero

    pl.when(jnp.logical_not(has_south))(lambda: blank(0))
    pl.when(jnp.logical_not(has_north))(lambda: blank(1))

    for copy in loads_rv + loads_s + [load_c]:
        copy.wait()
    mix = [[C[k, 0, j] for j in range(K)] for k in range(K)]

    def weigh(x, carry):
        for h in range(2):
            for part in range(2):
                rows = pl.ds(8 * part * X + x, 8, stride=X)
                out = pl.ds(8 * part, 8)
                speed = RV[1, h, rows, :]
                diag = 6.0 + RV[0, h, rows, :] + speed
                V1[h, x, out] = 1.0 + speed
                for k in range(K):
                    W[h, k, x, out] = OMEGA / (diag + mix[k][k])
                    SS[h, k, x, out] = S[h, k, rows, :]
        return carry

    lax.fori_loop(0, X, weigh, 0)

    ghosts.wait()
    own = jnp.where(fluid, 0.0, 1.0)

    def ghost(h, k, x, layer):
        return own * layer + GH[h, k, pl.ds(x, 1), :]

    def frame(x, carry):
        for h in range(2):
            for k in range(K):
                for t in range(SWEEPS):
                    U[t, x + 1, h, k, pl.ds(8 + L, 8)] = zero
                U[0, x + 1, h, k, 7:8] = ghost(h, k, x, U[0, x + 1, h, k, 8:9])
        return carry

    lax.fori_loop(0, X, frame, 0)

    for g, h in quarters:
        weights = zero
        for x, number in rows_of(g):
            for k in range(K):
                for part, slot in enumerate(slots(number, k)):
                    weights = packed(weights, W[h, k, x, pl.ds(8 * part, 8)], h, slot)
        WP[g, h] = weights

    def share(packet, x, number, h, k, part):
        beyond = unpacked(packet, h, slots(number, k)[part])
        return jnp.where(lane == h * (LANES - 1), W[h, k, x, pl.ds(8 * part, 8)] * beyond, 0.0)

    def relax(t, x, h):
        tiles = [pl.ds(8 * part, 8) for part in range(2)]
        outer, inner = ((0, LANES - 1), (LANES - 1, 0))[h]
        away, back = ((1, LANES - 1), (LANES - 1, 1))[h]

        def state(x, h, k, part, up=0):
            return U[t, x + 1, h, k, pl.ds(8 + 8 * part + up, 8)]

        for part in range(2):
            speed = V1[h, x, tiles[part]]
            center = [state(x, h, k, part) for k in range(K)]
            for k in range(K):
                here = center[k]
                outwards = jnp.where(lane == outer, 0.0, pltpu.roll(here, away, 1))
                across = jnp.where(lane == outer, state(x, 1 - h, k, part), here)
                inwards = pltpu.roll(across, back, 1)
                total = SS[h, k, x, tiles[part]] + state(x, h, k, part, -1) + state(x, h, k, part, 1)
                total = total + speed * state(x - 1, h, k, part) + state(x + 1, h, k, part)
                total = total + outwards + inwards
                for j in range(K):
                    if j != k:
                        total = total - mix[k][j] * center[j]
                yield k, part, (1.0 - OMEGA) * here + W[h, k, x, tiles[part]] * total

    def gather(t, h, rows, packet):
        for x, number in rows:
            for k in range(K):
                for part, slot in enumerate(slots(number, k)):
                    packet = packed(packet, U[t, x + 1, h, k, pl.ds(8 + 8 * part, 8)], h, slot)
        return packet

    def advance(t, x, h):
        for k, part, new in relax(t, x, h):
            U[t + 1, x + 1, h, k, pl.ds(8 + 8 * part, 8)] = new
            if part == 0:
                U[t + 1, x + 1, h, k, 7:8] = ghost(h, k, x, new[0:1])

    def sweep(t, carry):
        packets = {}
        for g, h in quarters:
            inner = rows_of(g)[1:]
            for x, _ in inner:
                advance(t, x, h)
            packets[g, h] = gather(t + 1, h, inner, zero)
        for g, h in quarters:
            edge = rows_of(g)[:1]
            x_copy(t, 1 - g, h).wait_recv()
            advance(t, edge[0][0], h)
            packet = gather(t + 1, h, edge, packets[g, h])
            y_wait(t, g, h)
            beyond = YI[t, g, h]
            YO[t + 1, g, 1 - h] = packet + WP[g, h] * beyond
            y_start(t + 1, g, h)
            for x, number in rows_of(g):
                for k in range(K):
                    for part in range(2):
                        more = share(beyond, x, number, h, k, part)
                        U[t + 1, x + 1, h, k, pl.ds(8 + 8 * part, 8)] += more
                        if part == 0:
                            U[t + 1, x + 1, h, k, 7:8] += own * more[0:1]
                if number == 0:
                    x_copy(t + 1, g, h).start()
        sent(t)
        return carry

    lax.fori_loop(0, SWEEPS - 1, sweep, 0)

    last = SWEEPS - 1
    half_rows = X // 2

    def trace(g, h):
        rows = pl.ds((1 - g) * half_rows, half_rows)
        return pltpu.make_async_remote_copy(
            O.at[h, :, rows],
            PR.at[h, :, rows],
            ts_sem.at[g, h],
            tr_sem.at[g, h],
            device_id=partner,
            device_id_type=MESH,
        )

    def conclude(x, h):
        for k, part, new in relax(last, x, h):
            O[h, k, pl.ds(8 * part * X + x, 8, stride=X), :] = new

    for g, h in quarters:
        for x, _ in rows_of(g)[1:]:
            conclude(x, h)
    for g, h in quarters:
        x_copy(last, 1 - g, h).wait_recv()
        conclude(rows_of(g)[0][0], h)
        y_wait(last, g, h)
        beyond = YI[last, g, h]
        for part in range(2):
            for x, number in rows_of(g):
                for k in range(K):
                    rows = pl.ds(8 * part * X + x, 8, stride=X)
                    O[h, k, rows, :] += share(beyond, x, number, h, k, part)
            if part == 0:
                trace(g, h).start()
    sent(last)
    mine = jnp.where(fluid, 1.0 - THETA, THETA)
    other = jnp.where(fluid, THETA, 1.0 - THETA)
    for g, h in quarters:
        trace(g, h).wait()
        rows = pl.ds((1 - g) * half_rows, half_rows)
        for k in range(K):
            IO[h, k, rows] = mine * O[h, k, rows] + other * PR[h, k, rows]


def write(a_ref, b_ref, o_ref, i_ref, sem):
    copies = [
        pltpu.make_async_copy(
            tile_ref.at[h], out_ref.at[..., pl.ds(h * LANES, LANES)], sem.at[n, h]
        )
        for n, (tile_ref, out_ref) in enumerate(((a_ref, o_ref), (b_ref, i_ref)))
        for h in range(2)
    ]
    for copy in copies:
        copy.start()
    for copy in copies:
        copy.wait()


def solution(mesh):
    nx, ny = mesh.shape["gx"], mesh.shape["gy"]

    def local(fields, source, reaction, velocity, coupling):
        _, _, L, X, Y = fields.shape
        groups = 2
        f32 = jnp.float32
        cells = L * X
        tiles, edges = pl.pallas_call(
            functools.partial(kernel, nx, ny, L, X),
            out_shape=(
                pltpu.VMEM((2, K, cells, LANES), f32),
                pltpu.VMEM((2, K, X, LANES), f32),
            ),
            in_specs=[pl.BlockSpec(memory_space=pltpu.HBM)] * 5,
            out_specs=[pl.BlockSpec(memory_space=pltpu.VMEM)] * 2,
            scratch_shapes=[
                pltpu.VMEM((2, K, cells, LANES), f32),
                pltpu.VMEM((2, K, cells, LANES), f32),
                pltpu.VMEM((2, 2, cells, LANES), f32),
                pltpu.VMEM((SWEEPS, X + 2, 2, K, L + 16, LANES), f32),
                pltpu.VMEM((2, K, X, L, LANES), f32),
                pltpu.VMEM((2, X, L, LANES), f32),
                pltpu.VMEM((2, K, X, L, LANES), f32),
                pltpu.VMEM((SWEEPS, groups, 2, 8, LANES), f32),
                pltpu.VMEM((SWEEPS, groups, 2, 8, LANES), f32),
                pltpu.VMEM((2, K, X, LANES), f32),
                pltpu.VMEM((2, K, X, LANES), f32),
                pltpu.VMEM((2, K, X, LANES), f32),
                pltpu.SemaphoreType.DMA((2,)),
                pltpu.SemaphoreType.DMA((2,)),
                pltpu.SemaphoreType.DMA((2, 2)),
                pltpu.SemaphoreType.DMA((SWEEPS, 2, 2)),
                pltpu.SemaphoreType.DMA((SWEEPS, 2, 2)),
                pltpu.SemaphoreType.DMA((SWEEPS, groups, 2)),
                pltpu.SemaphoreType.DMA((SWEEPS, groups, 2)),
                pltpu.SemaphoreType.DMA((2,)),
                pltpu.SemaphoreType.DMA((2, 2)),
                pltpu.SemaphoreType.DMA((2, 2)),
                pltpu.SMEM((K, 1, K), f32),
                pltpu.SemaphoreType.DMA,
                pltpu.VMEM((2, 2, 8, LANES), f32),
            ],
            compiler_params=pltpu.CompilerParams(
                collective_id=0,
                has_side_effects=True,
                vmem_limit_bytes=60 * 1024 * 1024,
            ),
        )(
            fields.reshape(K, cells, Y),
            source.reshape(K, cells, Y),
            reaction.reshape(cells, Y),
            velocity.reshape(cells, Y),
            coupling.reshape(K, 1, K),
        )
        tiles, edges = (
            pltpu.with_memory_space_constraint(value, pltpu.VMEM) for value in (tiles, edges)
        )
        new, interface = pl.pallas_call(
            write,
            out_shape=(
                jax.ShapeDtypeStruct((K, cells, Y), f32),
                jax.ShapeDtypeStruct((K, X, Y), f32),
            ),
            in_specs=[pl.BlockSpec(memory_space=pltpu.VMEM)] * 2,
            out_specs=[pl.BlockSpec(memory_space=pltpu.HBM)] * 2,
            scratch_shapes=[pltpu.SemaphoreType.DMA((2, 2))],
        )(tiles, edges)
        return new.reshape(1, K, L, X, Y), interface[None]

    return jax.shard_map(
        local,
        mesh=mesh,
        in_specs=(
            P("side", None, None, "gx", "gy"),
            P("side", None, None, "gx", "gy"),
            P("side", None, "gx", "gy"),
            P("side", None, "gx", "gy"),
            P("side", None, None),
        ),
        out_specs=(P("side", None, None, "gx", "gy"), P("side", None, "gx", "gy")),
        check_vma=False,
    )
```
